32 devices in a mesh: dp: 2 (over y), ctx: 4 (over z), head: 4 (over x, core).
Axes of the slice: x: 2, y: 2, z: 4, core: 2. Of those that a mesh axis runs over, the one named last changes fastest.
Arguments:
- latent: bfloat16 [2, 512, 576], P('dp', 'ctx'), may hold values from -8 to 8
- q_nope: bfloat16 [2, 512, 2048], P('dp', 'ctx', 'head'), may hold values from -6 to 6
- q_rope: bfloat16 [2, 512, 1024], P('dp', 'ctx', 'head'), may hold values from -8 to 8
- grad_out: bfloat16 [2, 512, 2048], P('dp', 'ctx', 'head'), may hold values from -6 to 6
- w_uk: bfloat16 [512, 2048], P(None, 'head'), may hold values from -0.25 to 0.25
- w_uv: bfloat16 [512, 2048], P(None, 'head'), may hold values from -0.25 to 0.25
- stretch_order: int32 [8], replicated, may hold values from 0 to 7, as said below
Outputs:
- d_latent: float32 [2, 512, 576], P('dp', ('ctx', 'head'))
- d_q_nope: bfloat16 [2, 512, 2048], P('dp', 'ctx', 'head')
- d_q_rope: bfloat16 [2, 512, 1024], P('dp', 'ctx', 'head')
- d_w_uk: float32 [512, 2048], P(None, 'head')
- d_w_uv: float32 [512, 2048], P(None, 'head')
The draws below stay inside these ranges and needn't reach their ends.
Inputs may be any that keep to these rules, and one draw needn't show every extreme that they name: `stretch_order`: entries 2d and 2d+1 name the causal blocks of the two row blocks of the d-th block of 128 rows; all entries together are a permutation, and each such pair sums to 7.
All inputs are finite; a program needn't handle non-finite values.
Results may differ from the reference program's by a relative error of at most 0.02.
Values may be sent and summed in bfloat16 or wider, within the bound.
A program may use at most 64 MiB of HBM per device.

```python
import math
import jax
import jax.numpy as jnp
from jax import lax

D_LAT = 512
D_ROPE = 64
D_NOPE = 128
D_V = 128
HEADS_DEV = 4
TOK_DEV = 128
HEADS = 16
STRETCH = 64
SEQ = 512
N_DP = 2
N_CTX = 4
N_HEAD = 4


def draw_latent(key, part):
    key = jax.random.fold_in(key, 1)
    width = D_LAT + D_ROPE
    base = jnp.clip(jax.random.normal(key, (N_DP, SEQ, width)), -8.0, 8.0)
    return base.astype(jnp.bfloat16)


def draw_q_rope(key, part):
    key = jax.random.fold_in(key, 2)
    width = HEADS * D_ROPE
    base = jnp.clip(jax.random.normal(key, (N_DP, SEQ, width)), -8.0, 8.0)
    return base.astype(jnp.bfloat16)


def draw_stretch_order(key, part):
    key = jax.random.fold_in(key, 3)
    low_stretches = jax.random.permutation(key, N_CTX).astype(jnp.int32)
    paired = jnp.stack([low_stretches, 2 * N_CTX - 1 - low_stretches], axis=1)
    return paired.reshape(2 * N_CTX).astype(jnp.int32)


def levels(stream_key, extent, split, low, high):
    loudness = 1.0
    for position, blocks in split:
        steps = jax.random.uniform(jax.random.fold_in(jax.random.fold_in(stream_key, 6), position), (blocks,), jnp.float32, low / len(split), high / len(split))
        loudness = loudness * jnp.repeat(jnp.exp(steps), extent[position] // blocks).reshape((-1,) + (1,) * (len(extent) - 1 - position))
    return loudness


def scatter_about(own_key, shape, deviation, bound, shards=(), kind=jnp.bfloat16):
    loudness = levels(own_key, shape, shards, -0.22, 0.18) if shards else 1.0
    drawn = jax.random.normal(own_key, shape, jnp.float32) * deviation * loudness
    return jnp.minimum(jnp.maximum(drawn, -bound), bound).astype(kind)


def setup_inputs(seed: int = 0) -> dict:
    streams_of = jax.random.split(jax.random.key(seed), 8)
    return {
        "latent": draw_latent(jax.random.fold_in(streams_of[7], 71), 0),
        "q_nope": scatter_about(streams_of[1], (N_DP, SEQ, HEADS * D_NOPE), 1.0, 6.0, ((0, 2), (1, 4), (2, 4))),
        "q_rope": draw_q_rope(jax.random.fold_in(streams_of[7], 71), 0),
        "grad_out": scatter_about(streams_of[3], (N_DP, SEQ, HEADS * D_V), 1.0, 6.0, ((0, 2), (1, 4), (2, 4))),
        "w_uk": scatter_about(streams_of[4], (D_LAT, HEADS * D_NOPE), D_LAT ** -0.5, 0.25, ((1, 4),)),
        "w_uv": scatter_about(streams_of[5], (D_LAT, HEADS * D_V), D_LAT ** -0.5, 0.25, ((1, 4),)),
        "stretch_order": draw_stretch_order(jax.random.fold_in(streams_of[7], 71), 0),
    }


def position_table(stretch_order):
    row_index = jnp.arange(SEQ, dtype=jnp.int32)
    slot_index = 2 * (row_index // TOK_DEV) + row_index % TOK_DEV // STRETCH
    return stretch_order[slot_index] * STRETCH + row_index % STRETCH

def head_terms(key_rows, query_nope, query_rope, grad_head, key_weight, value_weight, allowed):
    score_scale = 1.0 / math.sqrt(D_NOPE + D_ROPE)
    query_latent = jnp.dot(query_nope, key_weight.T, preferred_element_type=jnp.float32).astype(jnp.bfloat16)
    query_cat = jnp.concatenate([query_latent, query_rope], axis=1)
    grad_latent = jnp.dot(grad_head, value_weight.T, preferred_element_type=jnp.float32).astype(jnp.bfloat16)
    latent_part = key_rows[:, :D_LAT]
    raw_score = jnp.dot(query_cat, key_rows.T, preferred_element_type=jnp.float32) * score_scale
    raw_score = jnp.where(allowed, raw_score, -jnp.inf)
    probability = jax.nn.softmax(raw_score, axis=1)
    prob_grad = jnp.dot(grad_latent, latent_part.T, preferred_element_type=jnp.float32)
    row_delta = lax.optimization_barrier(jnp.sum(probability * prob_grad, axis=1, keepdims=True))
    prob_low = probability.astype(jnp.bfloat16)
    score_grad = (score_scale * probability * (prob_grad - row_delta)).astype(jnp.bfloat16)
    output_latent = jnp.dot(prob_low, latent_part, preferred_element_type=jnp.float32).astype(jnp.bfloat16)
    query_grad = jnp.dot(score_grad, key_rows, preferred_element_type=jnp.float32)
    latent_query = query_grad[:, :D_LAT].astype(jnp.bfloat16)
    rope_grad = query_grad[:, D_LAT:].astype(jnp.bfloat16)
    nope_grad = jnp.dot(latent_query, key_weight, preferred_element_type=jnp.float32).astype(jnp.bfloat16)
    key_update = jnp.dot(latent_query.T, query_nope, preferred_element_type=jnp.float32)
    value_update = jnp.dot(output_latent.T, grad_head, preferred_element_type=jnp.float32)
    block_score = score_grad.astype(jnp.float32).reshape(N_CTX, TOK_DEV, SEQ)
    block_query = query_cat.astype(jnp.float32).reshape(N_CTX, TOK_DEV, D_LAT + D_ROPE)
    key_side = jnp.einsum('dtk,dtf->dkf', block_score, block_query)
    block_prob = prob_low.astype(jnp.float32).reshape(N_CTX, TOK_DEV, SEQ)
    block_grad = grad_latent.astype(jnp.float32).reshape(N_CTX, TOK_DEV, D_LAT)
    value_side = jnp.einsum('dtk,dtf->dkf', block_prob, block_grad)
    key_side = key_side.at[:, :, :D_LAT].add(value_side)
    return (key_side, nope_grad, rope_grad, key_update, value_update)

def reference(latent, q_nope, q_rope, grad_out, w_uk, w_uv, stretch_order):
    positions = position_table(stretch_order)
    allowed = positions[None, :] <= positions[:, None]
    latent_list, nope_list, rope_list = ([], [], [])
    key_total = jnp.zeros((D_LAT, HEADS * D_NOPE), jnp.float32)
    value_total = jnp.zeros((D_LAT, HEADS * D_V), jnp.float32)
    for replica in range(N_DP):
        key_rows = latent[replica]

        def group_step(latent_sum, group_index, key_rows=key_rows, replica=replica):
            nope_cols = lax.dynamic_slice_in_dim(q_nope[replica], group_index * (HEADS_DEV * D_NOPE), HEADS_DEV * D_NOPE, 1)
            rope_cols = lax.dynamic_slice_in_dim(q_rope[replica], group_index * (HEADS_DEV * D_ROPE), HEADS_DEV * D_ROPE, 1)
            grad_cols = lax.dynamic_slice_in_dim(grad_out[replica], group_index * (HEADS_DEV * D_V), HEADS_DEV * D_V, 1)
            key_cols = lax.dynamic_slice_in_dim(w_uk, group_index * (HEADS_DEV * D_NOPE), HEADS_DEV * D_NOPE, 1)
            value_cols = lax.dynamic_slice_in_dim(w_uv, group_index * (HEADS_DEV * D_V), HEADS_DEV * D_V, 1)
            group_side = jnp.zeros((N_CTX, SEQ, D_LAT + D_ROPE), jnp.float32)
            nope_parts, rope_parts, key_parts, value_parts = ([], [], [], [])
            for member in range(HEADS_DEV):
                results = head_terms(key_rows, nope_cols[:, member * D_NOPE:(member + 1) * D_NOPE], rope_cols[:, member * D_ROPE:(member + 1) * D_ROPE], grad_cols[:, member * D_V:(member + 1) * D_V], key_cols[:, member * D_NOPE:(member + 1) * D_NOPE], value_cols[:, member * D_V:(member + 1) * D_V], allowed)
                group_side = group_side + results[0]
                nope_parts.append(results[1])
                rope_parts.append(results[2])
                key_parts.append(results[3])
                value_parts.append(results[4])
            rounded = lax.optimization_barrier(group_side.astype(jnp.bfloat16)).astype(jnp.float32)
            latent_sum = latent_sum + lax.optimization_barrier(jnp.sum(rounded, axis=0))
            stacked = (jnp.concatenate(nope_parts, axis=1), jnp.concatenate(rope_parts, axis=1), jnp.concatenate(key_parts, axis=1), jnp.concatenate(value_parts, axis=1))
            return (latent_sum, stacked)
        latent_sum, stacked = lax.scan(group_step, jnp.zeros((SEQ, D_LAT + D_ROPE), jnp.float32), jnp.arange(N_HEAD, dtype=jnp.int32))
        latent_list.append(latent_sum)
        nope_list.append(stacked[0].transpose(1, 0, 2).reshape(SEQ, HEADS * D_NOPE))
        rope_list.append(stacked[1].transpose(1, 0, 2).reshape(SEQ, HEADS * D_ROPE))
        key_total = key_total + stacked[2].transpose(1, 0, 2).reshape(D_LAT, HEADS * D_NOPE)
        value_total = value_total + stacked[3].transpose(1, 0, 2).reshape(D_LAT, HEADS * D_V)
    return (jnp.stack(latent_list), jnp.stack(nope_list), jnp.stack(rope_list), key_total, value_total)
```

```python
import functools
import math

import jax
import jax.numpy as jnp
from jax import lax
from jax.experimental import pallas as pl
from jax.experimental.pallas import tpu as pltpu
from jax.sharding import PartitionSpec as P

D_LAT = 512
D_ROPE = 64
D_NOPE = 128
D_V = 128
TOK = 128
STRETCH = 64
WIDTH = D_LAT + D_ROPE
SCALE = 1.0 / math.sqrt(D_NOPE + D_ROPE)
MESH = pl.DeviceIdType.MESH
BF16 = jnp.bfloat16
F32 = jnp.float32


def dot_nn(a, b):
    return jnp.dot(a, b, preferred_element_type=F32)


def dot_nt(a, b):
    return lax.dot_general(a, b, (((1,), (1,)), ((), ())), preferred_element_type=F32)


def dot_tn(a, b):
    return lax.dot_general(a, b, (((0,), (0,)), ((), ())), preferred_element_type=F32)


def body(
    n_ctx, n_head, heads,
    lat, qn, qr, g, wk, wv, order,
    d_lat, d_qn, d_qr, d_wk, d_wv,
    gath, qc, gl, ql, key_pos, row_pos, pb, ds,
    wpart, yown, yrecv, zsend, zrecv, own, final, gsend, hrecv, lsend, lrecv,
    lat_s, lat_r, fwd_s, fwd_r, y_s, y_r, z_s, z_r, ag_s, ag_r, yag_s, yag_r, h_s, h_r, l_s, l_r,
    yown_s, zown_s, own_s, hown_s,
):
    rep = lax.axis_index("dp")
    ctx = lax.axis_index("ctx")
    head = lax.axis_index("head")
    other = 1 - rep
    half = lax.rem(head, 2)
    sibling = head + 1 - 2 * half

    def ctx_at(step):
        return lax.rem(ctx + step + n_ctx, n_ctx)

    def head_at(step):
        return lax.rem(head + step + n_head, n_head)

    def copy(src, dst, send, recv, target):
        return pltpu.make_async_remote_copy(
            src_ref=src, dst_ref=dst, send_sem=send, recv_sem=recv,
            device_id=target, device_id_type=MESH,
        )

    partners = [(rep, ctx_at(k), head) for k in range(1, n_ctx)]
    partners += [(rep, ctx, head_at(k)) for k in range(1, n_head)]
    partners += [(other, ctx, head)]
    barrier = pltpu.get_barrier_semaphore()
    for target in partners:
        pl.semaphore_signal(barrier, inc=1, device_id=target, device_id_type=MESH)
    pl.semaphore_wait(barrier, len(partners))

    sends = []

    def start(c):
        c.start()
        sends.append(c)
        return c

    def keep(src, dst, sem):
        c = pltpu.make_async_copy(src, dst, sem)
        c.start()
        return c

    lat_copies = [
        start(copy(lat.at[half], gath.at[k, half], lat_s.at[k - 1], lat_r.at[k - 1],
                   (rep, ctx_at(k), head)))
        for k in range(1, n_ctx)
    ]
    gath[0] = lat[...]

    def each(count, step):
        def run(i, carry):
            step(i)
            return carry

        lax.fori_loop(0, count, run, 0)

    def tile(m):
        return pl.ds(pl.multiple_of(m * 128, 128), 128)

    def project(m):
        rows = tile(m)
        qc[rows, :D_LAT] = dot_nt(qn[0, :, rows], wk[:, rows]).astype(BF16)
        gl[rows, :] = dot_nt(g[0, :, rows], wv[:, rows]).astype(BF16)

    each(heads, project)
    for m in range(heads):
        qc[m * TOK:(m + 1) * TOK, D_LAT:] = qr[0, :, m * D_ROPE:(m + 1) * D_ROPE]

    fwd_copies = []
    for k in range(1, n_ctx):
        lat_copies[k - 1].wait_recv()
        fwd_copies.append(
            start(copy(gath.at[k, half], gath.at[k, half], fwd_s.at[k - 1], fwd_r.at[k - 1],
                       (rep, ctx, sibling))))

    n_keys = n_ctx * TOK
    lane = lax.broadcasted_iota(jnp.int32, (1, n_keys), 1)
    start_pos = jnp.zeros((1, n_keys), jnp.int32)
    for k in range(n_ctx):
        owner = ctx_at(-k)
        for part in range(2):
            first = k * TOK + part * STRETCH
            inside = (lane >= first) & (lane < first + STRETCH)
            start_pos = start_pos + jnp.where(inside, order[2 * owner + part] * STRETCH, 0)
    key_pos[...] = start_pos + lane % STRETCH
    row = lax.broadcasted_iota(jnp.int32, (TOK, 1), 0)
    row_start = jnp.where(row < STRETCH, order[2 * ctx], order[2 * ctx + 1]) * STRETCH
    row_pos[...] = row_start + row % STRETCH

    for k in range(1, n_ctx):
        fwd_copies[k - 1].wait_recv()

    part_rows = wpart.shape[3]

    def weight_term(which, low, value, cols):
        term = dot_tn(low, value[0, :, cols]).astype(BF16)
        wpart[which, :, :, :, cols] = term.reshape(2, n_ctx, part_rows, 128)

    def send_half(which):
        return (
            keep(wpart.at[which, rep], yown.at[which], yown_s.at[which]),
            start(copy(wpart.at[which, other], yrecv.at[which], y_s.at[which], y_r.at[which],
                       (other, ctx, head))),
        )

    def attend(m):
        rows = tile(m)
        keys = gath[...].reshape(n_keys, WIDTH)
        score = dot_nt(qc[rows, :], keys) * SCALE
        score = jnp.where(key_pos[...] <= row_pos[...], score, -jnp.inf)
        expo = jnp.exp(score - jnp.max(score, axis=1, keepdims=True))
        prob = expo * (1.0 / jnp.sum(expo, axis=1, keepdims=True))
        low = prob.astype(BF16)
        pb[rows, :] = low
        grad = dot_nt(gl[rows, :], keys[:, :D_LAT])
        delta = jnp.sum(prob * grad, axis=1, keepdims=True)
        ds[rows, :] = (SCALE * prob * (grad - delta)).astype(BF16)
        out_low = dot_nn(low, keys[:, :D_LAT]).astype(BF16)
        weight_term(0, out_low, g, rows)

    each(heads, attend)
    y_copies = [send_half(0)]

    def query_side(m):
        rows = tile(m)
        keys = gath[...].reshape(n_keys, WIDTH)
        low = dot_nn(ds[rows, :], keys).astype(BF16)
        ql[rows, :] = low
        weight_term(1, low[:, :D_LAT], qn, rows)

    each(heads, query_side)
    y_copies.append(send_half(1))

    own_rows = TOK // n_head

    def key_side(k):
        cols = tile(k)
        value = dot_tn(pb[:, cols], gl[...])
        key = dot_tn(ds[:, cols], qc[...])
        low = key[:, :D_LAT] + value
        gsend[:, k, :, :D_LAT] = low.reshape(n_head, own_rows, D_LAT).astype(BF16)
        gsend[:, k, :, D_LAT:] = key[:, D_LAT:].reshape(n_head, own_rows, D_ROPE).astype(BF16)

    each(n_ctx, key_side)
    h_own = keep(gsend.at[head], hrecv.at[n_head - 1], hown_s.at[0])
    h_copies = [
        start(copy(gsend.at[head_at(k)], hrecv.at[k - 1], h_s.at[k - 1], h_r.at[k - 1],
                   (rep, ctx, head_at(k))))
        for k in range(1, n_head)
    ]

    def spread(which):
        y_copies[which][0].wait()
        y_copies[which][1].wait_recv()

        def add(i):
            total = yown[which, i].astype(F32) + yrecv[which, i].astype(F32)
            zsend[which, i] = total.astype(BF16)

        each(n_ctx, add)
        z_own.append(keep(zsend.at[which, ctx], zrecv.at[which, n_ctx - 1], zown_s.at[which]))
        return [
            start(copy(zsend.at[which, ctx_at(k)], zrecv.at[which, k - 1],
                       z_s.at[which, k - 1], z_r.at[which, k - 1], (rep, ctx_at(k), head)))
            for k in range(1, n_ctx)
        ]

    z_own = []
    z_copies = [spread(0)]

    def nope(m):
        rows = tile(m)
        d_qn[0, :, rows] = dot_nn(ql[rows, :D_LAT], wk[:, rows]).astype(BF16)

    each(heads, nope)
    for m in range(heads):
        d_qr[0, :, m * D_ROPE:(m + 1) * D_ROPE] = ql[m * TOK:(m + 1) * TOK, D_LAT:]
    z_copies.append(spread(1))

    h_own.wait()
    for c in h_copies:
        c.wait_recv()
    l_copies = []
    owned = None
    for k in range(n_ctx):
        total = hrecv[n_head - 1, k].astype(F32)
        for i in range(n_head - 1):
            total = total + hrecv[i, k].astype(F32)
        if k == 0:
            owned = total
        else:
            lsend[k - 1] = total.astype(BF16)
            l_copies.append(
                start(copy(lsend.at[k - 1], lrecv.at[k - 1], l_s.at[k - 1], l_r.at[k - 1],
                           (rep, ctx_at(-k), head))))

    ag_copies, yag_copies, own_copies = [], [], []
    for which in range(2):
        z_own[which].wait()
        for c in z_copies[which]:
            c.wait_recv()
        total = zrecv[which, n_ctx - 1].astype(F32)
        for k in range(1, n_ctx):
            total = total + zrecv[which, k - 1].astype(F32)
        own[which] = total.astype(BF16)
        mine = final.at[which, rep, ctx]
        own_copies.append(keep(own.at[which], mine, own_s.at[which]))
        ag_copies.append([
            start(copy(own.at[which], mine, ag_s.at[which, k - 1], ag_r.at[which, k - 1],
                       (rep, ctx_at(k), head)))
            for k in range(1, n_ctx)
        ])
        yag_copies.append([
            start(copy(own.at[which], mine, yag_s.at[which, 0], yag_r.at[which, 0], (other, ctx, head)))
        ])

    for c in l_copies:
        c.wait_recv()
    for k in range(1, n_ctx):
        owned = owned + lrecv[k - 1].astype(F32)
    d_lat[...] = owned

    for which in range(2):
        for k in range(1, n_ctx):
            there = final.at[which, rep, ctx_at(-k)]
            copy(there, there, ag_s.at[which, k - 1], ag_r.at[which, k - 1],
                 (rep, ctx_at(k), head)).wait_recv()
            yag_copies[which].append(
                start(copy(there, there, yag_s.at[which, k], yag_r.at[which, k],
                           (other, ctx, head))))
    for which, out in ((0, d_wv), (1, d_wk)):
        for k in range(n_ctx):
            there = final.at[which, other, ctx_at(-k)]
            copy(there, there, yag_s.at[which, k], yag_r.at[which, k],
                 (other, ctx, head)).wait_recv()
        own_copies[which].wait()

        def widen(i):
            first = pl.multiple_of(i * part_rows, part_rows)
            low = final[which, i // n_ctx, i % n_ctx]
            out[pl.ds(first, part_rows), :] = low.astype(F32)

        each(2 * n_ctx, widen)
    for c in sends:
        c.wait_send()


def local(n_ctx, n_head, latent, q_nope, q_rope, grad_out, w_uk, w_uv, stretch_order):
    heads = w_uk.shape[1] // D_NOPE
    rows = heads * TOK
    n_keys = n_ctx * TOK
    own = TOK // n_head
    part_rows = D_LAT // (2 * n_ctx)
    cols = w_uk.shape[1]
    vmem = pl.BlockSpec(memory_space=pltpu.VMEM)
    dma = pltpu.SemaphoreType.DMA
    outs = pl.pallas_call(
        functools.partial(body, n_ctx, n_head, heads),
        out_shape=(
            jax.ShapeDtypeStruct((own, WIDTH), F32),
            jax.ShapeDtypeStruct(q_nope.shape, BF16),
            jax.ShapeDtypeStruct(q_rope.shape, BF16),
            jax.ShapeDtypeStruct(w_uk.shape, F32),
            jax.ShapeDtypeStruct(w_uv.shape, F32),
        ),
        in_specs=[vmem] * 6 + [pl.BlockSpec(memory_space=pltpu.SMEM)],
        out_specs=(vmem,) * 5,
        scratch_shapes=[
            pltpu.VMEM((n_ctx, 2, TOK // 2, WIDTH), BF16),
            pltpu.VMEM((rows, WIDTH), BF16),
            pltpu.VMEM((rows, D_LAT), BF16),
            pltpu.VMEM((rows, WIDTH), BF16),
            pltpu.VMEM((1, n_keys), jnp.int32),
            pltpu.VMEM((TOK, 1), jnp.int32),
            pltpu.VMEM((rows, n_keys), BF16),
            pltpu.VMEM((rows, n_keys), BF16),
            pltpu.VMEM((2, 2, n_ctx, part_rows, cols), BF16),
            pltpu.VMEM((2, n_ctx, part_rows, cols), BF16),
            pltpu.VMEM((2, n_ctx, part_rows, cols), BF16),
            pltpu.VMEM((2, n_ctx, part_rows, cols), BF16),
            pltpu.VMEM((2, n_ctx, part_rows, cols), BF16),
            pltpu.VMEM((2, part_rows, cols), BF16),
            pltpu.VMEM((2, 2, n_ctx, part_rows, cols), BF16),
            pltpu.VMEM((n_head, n_ctx, own, WIDTH), BF16),
            pltpu.VMEM((n_head, n_ctx, own, WIDTH), BF16),
            pltpu.VMEM((n_ctx - 1, own, WIDTH), BF16),
            pltpu.VMEM((n_ctx - 1, own, WIDTH), BF16),
            dma((n_ctx - 1,)), dma((n_ctx - 1,)),
            dma((n_ctx - 1,)), dma((n_ctx - 1,)),
            dma((2,)), dma((2,)),
            dma((2, n_ctx - 1)), dma((2, n_ctx - 1)),
            dma((2, n_ctx - 1)), dma((2, n_ctx - 1)),
            dma((2, n_ctx)), dma((2, n_ctx)),
            dma((n_head - 1,)), dma((n_head - 1,)),
            dma((n_ctx - 1,)), dma((n_ctx - 1,)),
            dma((2,)), dma((2,)), dma((2,)), dma((1,)),
        ],
        compiler_params=pltpu.CompilerParams(
            collective_id=0, has_side_effects=True, vmem_limit_bytes=56 << 20
        ),
    )(latent.reshape(2, TOK // 2, WIDTH), q_nope, q_rope, grad_out, w_uk, w_uv, stretch_order)
    return (outs[0][None],) + tuple(outs[1:])


def solution(mesh):
    n_ctx, n_head = mesh.shape["ctx"], mesh.shape["head"]
    placed = (
        P("dp", "ctx", None),
        P("dp", "ctx", "head"),
        P("dp", "ctx", "head"),
        P("dp", "ctx", "head"),
        P(None, "head"),
        P(None, "head"),
        P(),
    )
    return jax.shard_map(
        functools.partial(local, n_ctx, n_head),
        mesh=mesh,
        in_specs=placed,
        out_specs=(
            P("dp", ("ctx", "head"), None),
            P("dp", "ctx", "head"),
            P("dp", "ctx", "head"),
            P(None, "head"),
            P(None, "head"),
        ),
        check_vma=False,
    )
```

```python
import functools
import math

import jax
import jax.numpy as jnp
from jax import lax
from jax.experimental import pallas as pl
from jax.experimental.pallas import tpu as pltpu
from jax.sharding import PartitionSpec as P

D_LAT = 512
D_ROPE = 64
D_NOPE = 128
D_V = 128
TOK = 128
STRETCH = 64
PAIR = 2
WIDTH = D_LAT + D_ROPE
SCALE = 1.0 / math.sqrt(D_NOPE + D_ROPE)
MESH = pl.DeviceIdType.MESH
BF16 = jnp.bfloat16
F32 = jnp.float32


def dot_nn(a, b):
    return jnp.dot(a, b, preferred_element_type=F32)


def dot_nt(a, b):
    return lax.dot_general(a, b, (((1,), (1,)), ((), ())), preferred_element_type=F32)


def dot_tn(a, b):
    return lax.dot_general(a, b, (((0,), (0,)), ((), ())), preferred_element_type=F32)


def body(
    n_ctx, n_head, groups,
    lat, qn, qr, g, wk, wv, order,
    d_lat, d_qn, d_qr, final,
    gath, qc, gl, ql, key_pos, row_pos, pb, ds,
    wpart, yown, yrecv, zsend, zrecv, own, gsend, hrecv, lsend, lrecv,
    lat_s, lat_r, fwd_s, fwd_r, y_s, y_r, z_s, z_r, ag_s, ag_r, yag_s, yag_r, h_s, h_r, l_s, l_r,
    yown_s, zown_s, own_s, hown_s,
):
    rep = lax.axis_index("dp")
    ctx = lax.axis_index("ctx")
    head = lax.axis_index("head")
    other = 1 - rep
    half = lax.rem(head, 2)
    sibling = head + 1 - 2 * half
    pieces = 2 * groups
    part_rows = own.shape[1]
    n_keys = n_ctx * TOK
    ctx_steps = range(1, n_ctx)

    def ctx_at(step):
        return lax.rem(ctx + step + n_ctx, n_ctx)

    def head_at(step):
        return lax.rem(head + step + n_head, n_head)

    def copy(src, dst, send, recv, target):
        return pltpu.make_async_remote_copy(
            src_ref=src, dst_ref=dst, send_sem=send, recv_sem=recv,
            device_id=target, device_id_type=MESH,
        )

    def each(first, last, step):
        def run(i, carry):
            step(i)
            return carry

        lax.fori_loop(first, last, run, 0)

    def tile(m, size):
        return pl.ds(pl.multiple_of(m * size, size), size)

    def lat_copy(k):
        cols = slice(k * TOK, (k + 1) * TOK)
        return copy(lat.at[half], gath.at[half, :, cols], lat_s.at[k - 1], lat_r.at[k - 1],
                    (rep, ctx_at(k), head))

    def fwd_copy(k):
        block = gath.at[half, :, slice(k * TOK, (k + 1) * TOK)]
        return copy(block, block, fwd_s.at[k - 1], fwd_r.at[k - 1], (rep, ctx, sibling))

    def y_copy(p):
        return copy(wpart.at[p, other], yrecv.at[p], y_s.at[p], y_r.at[p], (other, ctx, head))

    def y_keep(p):
        return pltpu.make_async_copy(wpart.at[p, rep], yown.at[p], yown_s.at[p])

    def z_copy(p, k):
        return copy(zsend.at[p, ctx_at(k)], zrecv.at[p, k - 1], z_s.at[p, k - 1], z_r.at[p, k - 1],
                    (rep, ctx_at(k), head))

    def z_keep(p):
        return pltpu.make_async_copy(zsend.at[p, ctx], zrecv.at[p, n_ctx - 1], zown_s.at[p])

    def ag_copy(p, k):
        return copy(own.at[p], final.at[p, rep, ctx], ag_s.at[p, k - 1], ag_r.at[p, k - 1],
                    (rep, ctx_at(k), head))

    def own_keep(p):
        return pltpu.make_async_copy(own.at[p], final.at[p, rep, ctx], own_s.at[p])

    def yag_copy(p, k):
        there = final.at[p, rep, ctx_at(-k)]
        return copy(own.at[p] if k == 0 else there, there, yag_s.at[p, k], yag_r.at[p, k],
                    (other, ctx, head))

    def h_copy(k):
        return copy(gsend.at[head_at(k)], hrecv.at[k - 1], h_s.at[k - 1], h_r.at[k - 1],
                    (rep, ctx, head_at(k)))

    def l_copy(k):
        return copy(lsend.at[k - 1], lrecv.at[k - 1], l_s.at[k - 1], l_r.at[k - 1],
                    (rep, ctx_at(-k), head))

    partners = [(rep, ctx_at(k), head) for k in ctx_steps]
    partners += [(rep, ctx, head_at(k)) for k in range(1, n_head)]
    partners += [(other, ctx, head)]
    barrier = pltpu.get_barrier_semaphore()
    for target in partners:
        pl.semaphore_signal(barrier, inc=1, device_id=target, device_id_type=MESH)
    pl.semaphore_wait(barrier, len(partners))

    for k in ctx_steps:
        lat_copy(k).start()
    gath[:, :, :TOK] = lat[...]

    def project(i):
        for sub in range(PAIR):
            rows = tile(i * PAIR + sub, 128)
            qc[rows, :D_LAT] = dot_nt(qn[0, :, rows], wk[:, rows]).astype(BF16)
            gl[rows, :] = dot_nt(g[0, :, rows], wv[:, rows]).astype(BF16)

    each(0, groups, project)
    for m in range(groups * PAIR):
        qc[m * TOK:(m + 1) * TOK, D_LAT:] = qr[0, :, m * D_ROPE:(m + 1) * D_ROPE]

    lane = lax.broadcasted_iota(jnp.int32, (1, n_keys), 1)
    start_pos = jnp.zeros((1, n_keys), jnp.int32)
    for k in range(n_ctx):
        owner = ctx_at(-k)
        for part in range(2):
            first = k * TOK + part * STRETCH
            inside = (lane >= first) & (lane < first + STRETCH)
            start_pos = start_pos + jnp.where(inside, order[2 * owner + part] * STRETCH, 0)
    key_pos[...] = start_pos + lane % STRETCH
    row = lax.broadcasted_iota(jnp.int32, (PAIR * TOK, 1), 0) % TOK
    row_start = jnp.where(row < STRETCH, order[2 * ctx], order[2 * ctx + 1]) * STRETCH
    row_pos[...] = row_start + row % STRETCH

    for k in ctx_steps:
        lat_copy(k).wait_recv()
        fwd_copy(k).start()
    for k in ctx_steps:
        fwd_copy(k).wait_recv()

    def weight_term(p, low, value, i):
        for sub in range(PAIR):
            cols = tile(i * PAIR + sub, 128)
            term = dot_tn(low[sub * TOK:(sub + 1) * TOK, :D_LAT], value[0, :, cols]).astype(BF16)
            wpart[p, :, :, :, sub * 128:(sub + 1) * 128] = term.reshape(2, n_ctx, part_rows, 128)
        y_keep(p).start()
        y_copy(p).start()

    def attend(i):
        rows = tile(i, PAIR * TOK)
        keys = gath[...].reshape(WIDTH, n_keys)
        score = dot_nn(qc[rows, :], keys) * SCALE
        score = jnp.where(key_pos[...] <= row_pos[...], score, -jnp.inf)
        expo = jnp.exp(score - jnp.max(score, axis=1, keepdims=True))
        prob = expo * (1.0 / jnp.sum(expo, axis=1, keepdims=True))
        low = prob.astype(BF16)
        pb[rows, :] = low
        grad = dot_nn(gl[rows, :], keys[:D_LAT, :])
        delta = jnp.sum(prob * grad, axis=1, keepdims=True)
        ds[rows, :] = (SCALE * prob * (grad - delta)).astype(BF16)
        out_low = dot_nt(low, keys[:D_LAT, :]).astype(BF16)
        weight_term(i, out_low, g, i)

    def spread(p):
        y_keep(p).wait()
        y_copy(p).wait_recv()

        def add(i):
            total = yown[p, i].astype(F32) + yrecv[p, i].astype(F32)
            zsend[p, i] = total.astype(BF16)

        each(0, n_ctx, add)
        z_keep(p).start()
        for k in ctx_steps:
            z_copy(p, k).start()

    def query_side(i):
        spread(i)
        rows = tile(i, PAIR * TOK)
        keys = gath[...].reshape(WIDTH, n_keys)
        low = dot_nt(ds[rows, :], keys).astype(BF16)
        ql[rows, :] = low
        weight_term(groups + i, low, qn, i)

    own_rows = TOK // n_head

    def key_side(k):
        cols = tile(k, TOK)
        value = dot_tn(pb[:, cols], gl[...])
        key = dot_tn(ds[:, cols], qc[...])
        low = key[:, :D_LAT] + value
        gsend[:, k, :, :D_LAT] = low.reshape(n_head, own_rows, D_LAT).astype(BF16)
        gsend[:, k, :, D_LAT:] = key[:, D_LAT:].reshape(n_head, own_rows, D_ROPE).astype(BF16)

    each(0, groups, attend)
    each(0, groups, query_side)
    for i in range(groups):
        each(i * n_ctx // groups, (i + 1) * n_ctx // groups, key_side)
        spread(groups + i)
    h_keep = pltpu.make_async_copy(gsend.at[head], hrecv.at[n_head - 1], hown_s.at[0])
    h_keep.start()
    for k in range(1, n_head):
        h_copy(k).start()

    def nope(i):
        for sub in range(PAIR):
            rows = tile(i * PAIR + sub, 128)
            d_qn[0, :, rows] = dot_nn(ql[rows, :D_LAT], wk[:, rows]).astype(BF16)

    each(0, groups, nope)
    for m in range(groups * PAIR):
        d_qr[0, :, m * D_ROPE:(m + 1) * D_ROPE] = ql[m * TOK:(m + 1) * TOK, D_LAT:]

    def settle(p):
        z_keep(p).wait()
        total = zrecv[p, n_ctx - 1].astype(F32)
        for k in ctx_steps:
            z_copy(p, k).wait_recv()
            total = total + zrecv[p, k - 1].astype(F32)
        own[p] = total.astype(BF16)
        for k in ctx_steps:
            ag_copy(p, k).start()
        yag_copy(p, 0).start()
        own_keep(p).start()

    def hand_on(p):
        for k in ctx_steps:
            there = final.at[p, rep, ctx_at(-k)]
            copy(there, there, ag_s.at[p, k - 1], ag_r.at[p, k - 1],
                 (rep, ctx_at(k), head)).wait_recv()
            yag_copy(p, k).start()

    def latent_terms():
        h_keep.wait()
        for k in range(1, n_head):
            h_copy(k).wait_recv()
        for k in range(n_ctx):
            total = hrecv[n_head - 1, k].astype(F32)
            for i in range(n_head - 1):
                total = total + hrecv[i, k].astype(F32)
            if k == 0:
                d_lat[...] = total
            else:
                lsend[k - 1] = total.astype(BF16)
                l_copy(k).start()

    for p in range(groups):
        settle(p)
    latent_terms()
    for p in range(groups):
        settle(groups + p)
        hand_on(p)
    for p in range(groups):
        hand_on(groups + p)
    total = d_lat[...]
    for k in ctx_steps:
        l_copy(k).wait_recv()
        total = total + lrecv[k - 1].astype(F32)
    d_lat[...] = total

    for k in ctx_steps:
        lat_copy(k).wait_send()
        fwd_copy(k).wait_send()
        l_copy(k).wait_send()
    for k in range(1, n_head):
        h_copy(k).wait_send()
    for p in range(pieces):
        y_copy(p).wait_send()
        own_keep(p).wait()
        for k in ctx_steps:
            z_copy(p, k).wait_send()
            ag_copy(p, k).wait_send()
        for k in range(n_ctx):
            there = final.at[p, other, ctx_at(-k)]
            arrived = copy(there, there, yag_s.at[p, k], yag_r.at[p, k], (other, ctx, head))
            arrived.wait_recv()
            yag_copy(p, k).wait_send()


def finish(groups, lat, qn, qr, weights, d_lat, d_qn, d_qr, d_wk, d_wv):
    d_lat[0] = lat[...]
    d_qn[...] = qn[...]
    d_qr[...] = qr[...]
    for which, out in ((0, d_wv), (1, d_wk)):
        for i in range(groups):
            value = weights[which * groups + i].reshape(D_LAT, PAIR * 128)
            out[:, i * PAIR * 128:(i + 1) * PAIR * 128] = value.astype(F32)


def local(n_ctx, n_head, latent, q_nope, q_rope, grad_out, w_uk, w_uv, stretch_order):
    heads = w_uk.shape[1] // D_NOPE
    groups = heads // PAIR
    pieces = 2 * groups
    rows = heads * TOK
    n_keys = n_ctx * TOK
    own = TOK // n_head
    part = (D_LAT // (2 * n_ctx), PAIR * 128)
    vmem = pl.BlockSpec(memory_space=pltpu.VMEM)
    dma = pltpu.SemaphoreType.DMA
    lat_out, qn_out, qr_out, weights = pl.pallas_call(
        functools.partial(body, n_ctx, n_head, groups),
        out_shape=(
            jax.ShapeDtypeStruct((own, WIDTH), F32),
            jax.ShapeDtypeStruct(q_nope.shape, BF16),
            jax.ShapeDtypeStruct(q_rope.shape, BF16),
            jax.ShapeDtypeStruct((pieces, 2, n_ctx) + part, BF16),
        ),
        in_specs=[vmem] * 6 + [pl.BlockSpec(memory_space=pltpu.SMEM)],
        out_specs=(vmem,) * 4,
        scratch_shapes=[
            pltpu.VMEM((2, WIDTH // 2, n_keys), BF16),
            pltpu.VMEM((rows, WIDTH), BF16),
            pltpu.VMEM((rows, D_LAT), BF16),
            pltpu.VMEM((rows, WIDTH), BF16),
            pltpu.VMEM((1, n_keys), jnp.int32),
            pltpu.VMEM((PAIR * TOK, 1), jnp.int32),
            pltpu.VMEM((rows, n_keys), BF16),
            pltpu.VMEM((rows, n_keys), BF16),
            pltpu.VMEM((pieces, 2, n_ctx) + part, BF16),
            pltpu.VMEM((pieces, n_ctx) + part, BF16),
            pltpu.VMEM((pieces, n_ctx) + part, BF16),
            pltpu.VMEM((pieces, n_ctx) + part, BF16),
            pltpu.VMEM((pieces, n_ctx) + part, BF16),
            pltpu.VMEM((pieces,) + part, BF16),
            pltpu.VMEM((n_head, n_ctx, own, WIDTH), BF16),
            pltpu.VMEM((n_head, n_ctx, own, WIDTH), BF16),
            pltpu.VMEM((n_ctx - 1, own, WIDTH), BF16),
            pltpu.VMEM((n_ctx - 1, own, WIDTH), BF16),
            dma((n_ctx - 1,)), dma((n_ctx - 1,)),
            dma((n_ctx - 1,)), dma((n_ctx - 1,)),
            dma((pieces,)), dma((pieces,)),
            dma((pieces, n_ctx - 1)), dma((pieces, n_ctx - 1)),
            dma((pieces, n_ctx - 1)), dma((pieces, n_ctx - 1)),
            dma((pieces, n_ctx)), dma((pieces, n_ctx)),
            dma((n_head - 1,)), dma((n_head - 1,)),
            dma((n_ctx - 1,)), dma((n_ctx - 1,)),
            dma((pieces,)), dma((pieces,)), dma((pieces,)), dma((1,)),
        ],
        compiler_params=pltpu.CompilerParams(
            collective_id=0, has_side_effects=True, vmem_limit_bytes=56 << 20
        ),
    )(latent.transpose(0, 2, 1).reshape(2, WIDTH // 2, TOK), q_nope, q_rope, grad_out, w_uk, w_uv,
      stretch_order)
    return pl.pallas_call(
        functools.partial(finish, groups),
        out_shape=(
            jax.ShapeDtypeStruct((1, own, WIDTH), F32),
            jax.ShapeDtypeStruct(q_nope.shape, BF16),
            jax.ShapeDtypeStruct(q_rope.shape, BF16),
            jax.ShapeDtypeStruct(w_uk.shape, F32),
            jax.ShapeDtypeStruct(w_uv.shape, F32),
        ),
        in_specs=[vmem] * 4,
        out_specs=(vmem,) * 5,
        compiler_params=pltpu.CompilerParams(vmem_limit_bytes=16 << 20),
    )(lat_out, qn_out, qr_out, weights)


def solution(mesh):
    n_ctx, n_head = mesh.shape["ctx"], mesh.shape["head"]
    placed = (
        P("dp", "ctx", None),
        P("dp", "ctx", "head"),
        P("dp", "ctx", "head"),
        P("dp", "ctx", "head"),
        P(None, "head"),
        P(None, "head"),
        P(),
    )
    return jax.shard_map(
        functools.partial(local, n_ctx, n_head),
        mesh=mesh,
        in_specs=placed,
        out_specs=(
            P("dp", ("ctx", "head"), None),
            P("dp", "ctx", "head"),
            P("dp", "ctx", "head"),
            P(None, "head"),
            P(None, "head"),
        ),
        check_vma=False,
    )
```

```python
import functools
import math

import jax
import jax.numpy as jnp
from jax import lax
from jax.experimental import pallas as pl
from jax.experimental.pallas import tpu as pltpu
from jax.sharding import PartitionSpec as P

D_LAT = 512
D_ROPE = 64
D_NOPE = 128
D_V = 128
TOK = 128
STRETCH = 64
PAIR = 1
WIDTH = D_LAT + D_ROPE
SCALE = 1.0 / math.sqrt(D_NOPE + D_ROPE)
MESH = pl.DeviceIdType.MESH
BF16 = jnp.bfloat16
F32 = jnp.float32


def dot_nn(a, b):
    return jnp.dot(a, b, preferred_element_type=F32)


def dot_nt(a, b):
    return lax.dot_general(a, b, (((1,), (1,)), ((), ())), preferred_element_type=F32)


def dot_tn(a, b):
    return lax.dot_general(a, b, (((0,), (0,)), ((), ())), preferred_element_type=F32)


def body(
    n_ctx, n_head, groups,
    lat, qn_in, qr_in, g_in, wk_in, wv_in, order,
    d_lat, d_qn, d_qr, final,
    qn, qr, g, wk, wv,
    gath, qc, gl, ql, key_pos, row_pos, pb, ds,
    wpart, yown, yrecv, zsend, zrecv, own, gsend, hrecv, lsend, lrecv,
    lat_s, lat_r, fwd_s, fwd_r, y_s, y_r, z_s, z_r, ag_s, ag_r, yag_s, yag_r, h_s, h_r, l_s, l_r,
    yown_s, zown_s, own_s, hown_s, in_s,
):
    rep = lax.axis_index("dp")
    ctx = lax.axis_index("ctx")
    head = lax.axis_index("head")
    other = 1 - rep
    half = lax.rem(head, 2)
    sibling = head + 1 - 2 * half
    pieces = 2 * groups
    part_rows = own.shape[1]
    n_keys = n_ctx * TOK
    ctx_steps = range(1, n_ctx)

    def ctx_at(step):
        return lax.rem(ctx + step + n_ctx, n_ctx)

    def head_at(step):
        return lax.rem(head + step + n_head, n_head)

    def copy(src, dst, send, recv, target):
        return pltpu.make_async_remote_copy(
            src_ref=src, dst_ref=dst, send_sem=send, recv_sem=recv,
            device_id=target, device_id_type=MESH,
        )

    def each(first, last, step):
        def run(i, carry):
            step(i)
            return carry

        lax.fori_loop(first, last, run, 0)

    def tile(m, size):
        return pl.ds(pl.multiple_of(m * size, size), size)

    def lat_copy(k):
        cols = slice(k * TOK, (k + 1) * TOK)
        return copy(lat.at[half], gath.at[half, :, cols], lat_s.at[k - 1], lat_r.at[k - 1],
                    (rep, ctx_at(k), head))

    def fwd_copy(k):
        block = gath.at[half, :, slice(k * TOK, (k + 1) * TOK)]
        return copy(block, block, fwd_s.at[k - 1], fwd_r.at[k - 1], (rep, ctx, sibling))

    def y_copy(p):
        return copy(wpart.at[p, other], yrecv.at[p], y_s.at[p], y_r.at[p], (other, ctx, head))

    def y_keep(p):
        return pltpu.make_async_copy(wpart.at[p, rep], yown.at[p], yown_s.at[p])

    def z_copy(p, k):
        return copy(zsend.at[p, ctx_at(k)], zrecv.at[p, k - 1], z_s.at[p, k - 1], z_r.at[p, k - 1],
                    (rep, ctx_at(k), head))

    def z_keep(p):
        return pltpu.make_async_copy(zsend.at[p, ctx], zrecv.at[p, n_ctx - 1], zown_s.at[p])

    def ag_copy(p, k):
        return copy(own.at[p], final.at[p, rep, ctx], ag_s.at[p, k - 1], ag_r.at[p, k - 1],
                    (rep, ctx_at(k), head))

    def own_keep(p):
        return pltpu.make_async_copy(own.at[p], final.at[p, rep, ctx], own_s.at[p])

    def yag_copy(p, k):
        there = final.at[p, rep, ctx_at(-k)]
        return copy(own.at[p] if k == 0 else there, there, yag_s.at[p, k], yag_r.at[p, k],
                    (other, ctx, head))

    def h_copy(k):
        return copy(gsend.at[head_at(k)], hrecv.at[k - 1], h_s.at[k - 1], h_r.at[k - 1],
                    (rep, ctx, head_at(k)))

    def l_copy(k):
        return copy(lsend.at[k - 1], lrecv.at[k - 1], l_s.at[k - 1], l_r.at[k - 1],
                    (rep, ctx_at(-k), head))

    fetches = [
        pltpu.make_async_copy(src, dst, in_s.at[i])
        for i, (src, dst) in enumerate((
            (lat, gath.at[:, :, :TOK]), (qn_in, qn), (wk_in, wk), (g_in, g), (wv_in, wv), (qr_in, qr),
        ))
    ]
    for c in fetches:
        c.start()

    partners = [(rep, ctx_at(k), head) for k in ctx_steps]
    partners += [(rep, ctx, head_at(k)) for k in range(1, n_head)]
    partners += [(other, ctx, head)]
    barrier = pltpu.get_barrier_semaphore()
    for target in partners:
        pl.semaphore_signal(barrier, inc=1, device_id=target, device_id_type=MESH)
    pl.semaphore_wait(barrier, len(partners))

    for k in ctx_steps:
        lat_copy(k).start()
    for c in fetches:
        c.wait()

    def project(i):
        for sub in range(PAIR):
            rows = tile(i * PAIR + sub, 128)
            qc[rows, :D_LAT] = dot_nt(qn[0, :, rows], wk[:, rows]).astype(BF16)
            gl[rows, :] = dot_nt(g[0, :, rows], wv[:, rows]).astype(BF16)

    each(0, groups, project)
    for m in range(groups * PAIR):
        qc[m * TOK:(m + 1) * TOK, D_LAT:] = qr[0, :, m * D_ROPE:(m + 1) * D_ROPE]

    lane = lax.broadcasted_iota(jnp.int32, (1, n_keys), 1)
    start_pos = jnp.zeros((1, n_keys), jnp.int32)
    for k in range(n_ctx):
        owner = ctx_at(-k)
        for part in range(2):
            first = k * TOK + part * STRETCH
            inside = (lane >= first) & (lane < first + STRETCH)
            start_pos = start_pos + jnp.where(inside, order[2 * owner + part] * STRETCH, 0)
    key_pos[...] = start_pos + lane % STRETCH
    row = lax.broadcasted_iota(jnp.int32, (PAIR * TOK, 1), 0) % TOK
    row_start = jnp.where(row < STRETCH, order[2 * ctx], order[2 * ctx + 1]) * STRETCH
    row_pos[...] = row_start + row % STRETCH

    for k in ctx_steps:
        lat_copy(k).wait_recv()
        fwd_copy(k).start()
    for k in ctx_steps:
        fwd_copy(k).wait_recv()

    def weight_term(p, low, value, i):
        for sub in range(PAIR):
            cols = tile(i * PAIR + sub, 128)
            term = dot_tn(low[sub * TOK:(sub + 1) * TOK, :D_LAT], value[0, :, cols]).astype(BF16)
            wpart[p, :, :, :, sub * 128:(sub + 1) * 128] = term.reshape(2, n_ctx, part_rows, 128)
        y_keep(p).start()
        y_copy(p).start()

    def spread(p):
        y_keep(p).wait()
        y_copy(p).wait_recv()

        def add(i):
            total = yown[p, i].astype(F32) + yrecv[p, i].astype(F32)
            zsend[p, i] = total.astype(BF16)

        each(0, n_ctx, add)
        z_keep(p).start()
        for k in ctx_steps:
            z_copy(p, k).start()

    def attend(i):
        pl.when(i >= 2)(lambda: spread(i - 2))
        rows = tile(i, PAIR * TOK)
        keys = gath[...].reshape(WIDTH, n_keys)
        score = dot_nn(qc[rows, :], keys) * SCALE
        score = jnp.where(key_pos[...] <= row_pos[...], score, -jnp.inf)
        expo = jnp.exp(score - jnp.max(score, axis=1, keepdims=True))
        prob = expo * (1.0 / jnp.sum(expo, axis=1, keepdims=True))
        low = prob.astype(BF16)
        pb[rows, :] = low
        grad = dot_nn(gl[rows, :], keys[:D_LAT, :])
        delta = jnp.sum(prob * grad, axis=1, keepdims=True)
        ds[rows, :] = (SCALE * prob * (grad - delta)).astype(BF16)
        out_low = dot_nt(low, keys[:D_LAT, :]).astype(BF16)
        weight_term(i, out_low, g, i)

    def query_side(i):
        spread(groups + i - 2)
        rows = tile(i, PAIR * TOK)
        keys = gath[...].reshape(WIDTH, n_keys)
        low = dot_nt(ds[rows, :], keys).astype(BF16)
        ql[rows, :] = low
        weight_term(groups + i, low, qn, i)

    own_rows = TOK // n_head

    def key_side(k):
        cols = tile(k, TOK)
        value = dot_tn(pb[:, cols], gl[...])
        key = dot_tn(ds[:, cols], qc[...])
        low = key[:, :D_LAT] + value
        gsend[:, k, :, :D_LAT] = low.reshape(n_head, own_rows, D_LAT).astype(BF16)
        gsend[:, k, :, D_LAT:] = key[:, D_LAT:].reshape(n_head, own_rows, D_ROPE).astype(BF16)

    each(0, groups, attend)
    each(0, groups, query_side)
    for i in range(2):
        each(i * n_ctx // 2, (i + 1) * n_ctx // 2, key_side)
        spread(pieces - 2 + i)
    h_keep = pltpu.make_async_copy(gsend.at[head], hrecv.at[n_head - 1], hown_s.at[0])
    h_keep.start()
    for k in range(1, n_head):
        h_copy(k).start()

    def nope(i):
        for sub in range(PAIR):
            rows = tile(i * PAIR + sub, 128)
            d_qn[0, :, rows] = dot_nn(ql[rows, :D_LAT], wk[:, rows]).astype(BF16)

    each(0, groups, nope)
    for m in range(groups * PAIR):
        d_qr[0, :, m * D_ROPE:(m + 1) * D_ROPE] = ql[m * TOK:(m + 1) * TOK, D_LAT:]

    def settle(p):
        z_keep(p).wait()
        total = zrecv[p, n_ctx - 1].astype(F32)
        for k in ctx_steps:
            z_copy(p, k).wait_recv()
            total = total + zrecv[p, k - 1].astype(F32)
        own[p] = total.astype(BF16)
        for k in ctx_steps:
            ag_copy(p, k).start()
        yag_copy(p, 0).start()
        own_keep(p).start()

    def hand_on(p):
        for k in ctx_steps:
            there = final.at[p, rep, ctx_at(-k)]
            copy(there, there, ag_s.at[p, k - 1], ag_r.at[p, k - 1],
                 (rep, ctx_at(k), head)).wait_recv()
            yag_copy(p, k).start()

    def latent_terms():
        h_keep.wait()
        for k in range(1, n_head):
            h_copy(k).wait_recv()
        for k in range(n_ctx):
            total = hrecv[n_head - 1, k].astype(F32)
            for i in range(n_head - 1):
                total = total + hrecv[i, k].astype(F32)
            if k == 0:
                d_lat[...] = total
            else:
                lsend[k - 1] = total.astype(BF16)
                l_copy(k).start()

    def settle_next(p):
        settle(p)
        hand_on(p - groups)

    each(0, groups, settle)
    latent_terms()
    each(groups, pieces, settle_next)
    each(groups, pieces, hand_on)
    total = d_lat[...]
    for k in ctx_steps:
        l_copy(k).wait_recv()
        total = total + lrecv[k - 1].astype(F32)
    d_lat[...] = total

    for k in ctx_steps:
        lat_copy(k).wait_send()
        fwd_copy(k).wait_send()
        l_copy(k).wait_send()
    for k in range(1, n_head):
        h_copy(k).wait_send()

    def end(p):
        y_copy(p).wait_send()
        own_keep(p).wait()
        for k in ctx_steps:
            z_copy(p, k).wait_send()
            ag_copy(p, k).wait_send()
        for k in range(n_ctx):
            there = final.at[p, other, ctx_at(-k)]
            arrived = copy(there, there, yag_s.at[p, k], yag_r.at[p, k], (other, ctx, head))
            arrived.wait_recv()
            yag_copy(p, k).wait_send()

    each(0, pieces, end)


def finish(groups, lat, qn, qr, weights, d_lat, d_qn, d_qr, d_wk, d_wv, sems):
    moves = [
        pltpu.make_async_copy(src, dst, sems.at[i])
        for i, (src, dst) in enumerate(((lat, d_lat.at[0]), (qn, d_qn), (qr, d_qr)))
    ]
    for c in moves:
        c.start()
    for which, out in ((0, d_wv), (1, d_wk)):
        for i in range(groups):
            value = weights[which * groups + i].reshape(D_LAT, PAIR * 128)
            out[:, i * PAIR * 128:(i + 1) * PAIR * 128] = value.astype(F32)
    for c in moves:
        c.wait()


def local(n_ctx, n_head, latent, q_nope, q_rope, grad_out, w_uk, w_uv, stretch_order):
    heads = w_uk.shape[1] // D_NOPE
    groups = heads // PAIR
    pieces = 2 * groups
    rows = heads * TOK
    n_keys = n_ctx * TOK
    own = TOK // n_head
    part = (D_LAT // (2 * n_ctx), PAIR * 128)
    vmem = pl.BlockSpec(memory_space=pltpu.VMEM)
    anywhere = pl.BlockSpec(memory_space=pl.ANY)
    dma = pltpu.SemaphoreType.DMA
    lat_out, qn_out, qr_out, weights = pl.pallas_call(
        functools.partial(body, n_ctx, n_head, groups),
        out_shape=(
            jax.ShapeDtypeStruct((own, WIDTH), F32),
            jax.ShapeDtypeStruct(q_nope.shape, BF16),
            jax.ShapeDtypeStruct(q_rope.shape, BF16),
            jax.ShapeDtypeStruct((pieces, 2, n_ctx) + part, BF16),
        ),
        in_specs=[anywhere] * 6 + [pl.BlockSpec(memory_space=pltpu.SMEM)],
        out_specs=(vmem,) * 4,
        scratch_shapes=[
            pltpu.VMEM(q_nope.shape, BF16),
            pltpu.VMEM(q_rope.shape, BF16),
            pltpu.VMEM(grad_out.shape, BF16),
            pltpu.VMEM(w_uk.shape, BF16),
            pltpu.VMEM(w_uv.shape, BF16),
            pltpu.VMEM((2, WIDTH // 2, n_keys), BF16),
            pltpu.VMEM((rows, WIDTH), BF16),
            pltpu.VMEM((rows, D_LAT), BF16),
            pltpu.VMEM((rows, WIDTH), BF16),
            pltpu.VMEM((1, n_keys), jnp.int32),
            pltpu.VMEM((PAIR * TOK, 1), jnp.int32),
            pltpu.VMEM((rows, n_keys), BF16),
            pltpu.VMEM((rows, n_keys), BF16),
            pltpu.VMEM((pieces, 2, n_ctx) + part, BF16),
            pltpu.VMEM((pieces, n_ctx) + part, BF16),
            pltpu.VMEM((pieces, n_ctx) + part, BF16),
            pltpu.VMEM((pieces, n_ctx) + part, BF16),
            pltpu.VMEM((pieces, n_ctx) + part, BF16),
            pltpu.VMEM((pieces,) + part, BF16),
            pltpu.VMEM((n_head, n_ctx, own, WIDTH), BF16),
            pltpu.VMEM((n_head, n_ctx, own, WIDTH), BF16),
            pltpu.VMEM((n_ctx - 1, own, WIDTH), BF16),
            pltpu.VMEM((n_ctx - 1, own, WIDTH), BF16),
            dma((n_ctx - 1,)), dma((n_ctx - 1,)),
            dma((n_ctx - 1,)), dma((n_ctx - 1,)),
            dma((pieces,)), dma((pieces,)),
            dma((pieces, n_ctx - 1)), dma((pieces, n_ctx - 1)),
            dma((pieces, n_ctx - 1)), dma((pieces, n_ctx - 1)),
            dma((pieces, n_ctx)), dma((pieces, n_ctx)),
            dma((n_head - 1,)), dma((n_head - 1,)),
            dma((n_ctx - 1,)), dma((n_ctx - 1,)),
            dma((pieces,)), dma((pieces,)), dma((pieces,)), dma((1,)), dma((6,)),
        ],
        compiler_params=pltpu.CompilerParams(
            collective_id=0, has_side_effects=True, vmem_limit_bytes=56 << 20
        ),
    )(latent.transpose(0, 2, 1).reshape(2, WIDTH // 2, TOK), q_nope, q_rope, grad_out, w_uk, w_uv,
      stretch_order)
    return pl.pallas_call(
        functools.partial(finish, groups),
        out_shape=(
            jax.ShapeDtypeStruct((1, own, WIDTH), F32),
            jax.ShapeDtypeStruct(q_nope.shape, BF16),
            jax.ShapeDtypeStruct(q_rope.shape, BF16),
            jax.ShapeDtypeStruct(w_uk.shape, F32),
            jax.ShapeDtypeStruct(w_uv.shape, F32),
        ),
        in_specs=[anywhere] * 3 + [vmem],
        out_specs=(anywhere,) * 3 + (vmem,) * 2,
        scratch_shapes=[dma((3,))],
        compiler_params=pltpu.CompilerParams(vmem_limit_bytes=60 << 20),
    )(lat_out, qn_out, qr_out, weights)


def solution(mesh):
    n_ctx, n_head = mesh.shape["ctx"], mesh.shape["head"]
    placed = (
        P("dp", "ctx", None),
        P("dp", "ctx", "head"),
        P("dp", "ctx", "head"),
        P("dp", "ctx", "head"),
        P(None, "head"),
        P(None, "head"),
        P(),
    )
    return jax.shard_map(
        functools.partial(local, n_ctx, n_head),
        mesh=mesh,
        in_specs=placed,
        out_specs=(
            P("dp", ("ctx", "head"), None),
            P("dp", "ctx", "head"),
            P("dp", "ctx", "head"),
            P(None, "head"),
            P(None, "head"),
        ),
        check_vma=False,
    )
```

```python
import functools
import math

import jax
import jax.numpy as jnp
from jax import lax
from jax.experimental import pallas as pl
from jax.experimental.pallas import tpu as pltpu
from jax.sharding import PartitionSpec as P

D_LAT = 512
D_ROPE = 64
D_NOPE = 128
D_V = 128
TOK = 128
STRETCH = 64
PAIR = 2
WIDTH = D_LAT + D_ROPE
SCALE = 1.0 / math.sqrt(D_NOPE + D_ROPE)
MESH = pl.DeviceIdType.MESH
BF16 = jnp.bfloat16
F32 = jnp.float32


def dot_nn(a, b):
    return jnp.dot(a, b, preferred_element_type=F32)


def dot_nt(a, b):
    return lax.dot_general(a, b, (((1,), (1,)), ((), ())), preferred_element_type=F32)


def dot_tn(a, b):
    return lax.dot_general(a, b, (((0,), (0,)), ((), ())), preferred_element_type=F32)


def body(
    n_ctx, n_head, groups,
    lat, qn_in, qr_in, g_in, wk_in, wv_in, order,
    d_lat, d_qn, d_qr, final,
    qn, qr, g, wk, wv,
    gath, keys_n, qc, gl, qct, glt, qlt, bias, pbt, dst,
    wpart, yown, yrecv, zsend, zrecv, own, gsend, hrecv, lsend, lrecv,
    lat_s, lat_r, fwd_s, fwd_r, y_s, y_r, z_s, z_r, ag_s, ag_r, yag_s, yag_r, h_s, h_r, l_s, l_r,
    yown_s, zown_s, own_s, hown_s, in_s,
):
    rep = lax.axis_index("dp")
    ctx = lax.axis_index("ctx")
    head = lax.axis_index("head")
    other = 1 - rep
    half = lax.rem(head, 2)
    sibling = head + 1 - 2 * half
    pieces = 2 * groups
    part_rows = own.shape[1]
    n_keys = n_ctx * TOK
    ctx_steps = range(1, n_ctx)

    def ctx_at(step):
        return lax.rem(ctx + step + n_ctx, n_ctx)

    def head_at(step):
        return lax.rem(head + step + n_head, n_head)

    def copy(src, dst, send, recv, target):
        return pltpu.make_async_remote_copy(
            src_ref=src, dst_ref=dst, send_sem=send, recv_sem=recv,
            device_id=target, device_id_type=MESH,
        )

    def each(first, last, step):
        def run(i, carry):
            step(i)
            return carry

        lax.fori_loop(first, last, run, 0)

    def tile(m, size):
        return pl.ds(pl.multiple_of(m * size, size), size)

    def lat_copy(k):
        cols = slice(k * TOK, (k + 1) * TOK)
        return copy(lat.at[half], gath.at[half, :, cols], lat_s.at[k - 1], lat_r.at[k - 1],
                    (rep, ctx_at(k), head))

    def fwd_copy(k):
        block = gath.at[half, :, slice(k * TOK, (k + 1) * TOK)]
        return copy(block, block, fwd_s.at[k - 1], fwd_r.at[k - 1], (rep, ctx, sibling))

    def y_copy(p):
        return copy(wpart.at[p, other], yrecv.at[p], y_s.at[p], y_r.at[p], (other, ctx, head))

    def y_keep(p):
        return pltpu.make_async_copy(wpart.at[p, rep], yown.at[p], yown_s.at[p])

    def z_copy(p, k):
        return copy(zsend.at[p, ctx_at(k)], zrecv.at[p, k - 1], z_s.at[p, k - 1], z_r.at[p, k - 1],
                    (rep, ctx_at(k), head))

    def z_keep(p):
        return pltpu.make_async_copy(zsend.at[p, ctx], zrecv.at[p, n_ctx - 1], zown_s.at[p])

    def ag_copy(p, k):
        return copy(own.at[p], final.at[p, rep, ctx], ag_s.at[p, k - 1], ag_r.at[p, k - 1],
                    (rep, ctx_at(k), head))

    def own_keep(p):
        return pltpu.make_async_copy(own.at[p], final.at[p, rep, ctx], own_s.at[p])

    def yag_copy(p, k):
        there = final.at[p, rep, ctx_at(-k)]
        return copy(own.at[p] if k == 0 else there, there, yag_s.at[p, k], yag_r.at[p, k],
                    (other, ctx, head))

    def h_copy(k):
        return copy(gsend.at[head_at(k)], hrecv.at[k - 1], h_s.at[k - 1], h_r.at[k - 1],
                    (rep, ctx, head_at(k)))

    def l_copy(k):
        return copy(lsend.at[k - 1], lrecv.at[k - 1], l_s.at[k - 1], l_r.at[k - 1],
                    (rep, ctx_at(-k), head))

    fetches = [
        pltpu.make_async_copy(src, dst, in_s.at[i])
        for i, (src, dst) in enumerate((
            (lat, gath.at[:, :, :TOK]), (qn_in, qn), (wk_in, wk), (g_in, g), (wv_in, wv), (qr_in, qr),
        ))
    ]
    for c in fetches:
        c.start()

    partners = [(rep, ctx_at(k), head) for k in ctx_steps]
    partners += [(rep, ctx, head_at(k)) for k in range(1, n_head)]
    partners += [(other, ctx, head)]
    barrier = pltpu.get_barrier_semaphore()
    for target in partners:
        pl.semaphore_signal(barrier, inc=1, device_id=target, device_id_type=MESH)
    pl.semaphore_wait(barrier, len(partners))

    for k in ctx_steps:
        lat_copy(k).start()
    for c in fetches:
        c.wait()

    def project(i):
        for sub in range(PAIR):
            rows = tile(i * PAIR + sub, 128)
            qn_h, g_h, wk_h, wv_h = qn[0, :, rows], g[0, :, rows], wk[:, rows], wv[:, rows]
            qc[rows, :D_LAT] = dot_nt(qn_h, wk_h).astype(BF16)
            gl[rows, :] = dot_nt(g_h, wv_h).astype(BF16)
            qct[:D_LAT, rows] = dot_nt(wk_h, qn_h).astype(BF16)
            glt[:, rows] = dot_nt(wv_h, g_h).astype(BF16)

    each(0, groups, project)
    rope_t = qr[0].T
    for m in range(groups * PAIR):
        rows, cols = slice(m * TOK, (m + 1) * TOK), slice(m * D_ROPE, (m + 1) * D_ROPE)
        qc[rows, D_LAT:] = qr[0, :, cols]
        qct[D_LAT:, rows] = rope_t[cols, :]

    lane = lax.broadcasted_iota(jnp.int32, (1, PAIR * TOK), 1) % TOK
    row_start = jnp.where(lane < STRETCH, order[2 * ctx], order[2 * ctx + 1]) * STRETCH
    row_pos = row_start + lane % STRETCH
    inner = lax.broadcasted_iota(jnp.int32, (STRETCH, PAIR * TOK), 0)
    for k in range(n_ctx):
        owner = ctx_at(-k)
        for part in range(2):
            key_pos = inner + order[2 * owner + part] * STRETCH
            first = k * TOK + part * STRETCH
            bias[first:first + STRETCH, :] = jnp.where(key_pos <= row_pos, 0.0, -jnp.inf)

    def turn(k):
        rows = slice(k * TOK, (k + 1) * TOK)
        keys_n[rows, :] = gath[:, :, rows].reshape(WIDTH, TOK).T

    turn(0)
    for k in ctx_steps:
        lat_copy(k).wait_recv()
        fwd_copy(k).start()
    for k in ctx_steps:
        fwd_copy(k).wait_recv()
        turn(k)

    def weight_term(p, low, value, i):
        for sub in range(PAIR):
            cols = tile(i * PAIR + sub, 128)
            term = dot_nn(low[:D_LAT, sub * TOK:(sub + 1) * TOK], value[0, :, cols]).astype(BF16)
            wpart[p, :, :, :, sub * 128:(sub + 1) * 128] = term.reshape(2, n_ctx, part_rows, 128)
        y_keep(p).start()
        y_copy(p).start()

    def spread(p):
        y_keep(p).wait()
        y_copy(p).wait_recv()

        def add(i):
            total = yown[p, i].astype(F32) + yrecv[p, i].astype(F32)
            zsend[p, i] = total.astype(BF16)

        each(0, n_ctx, add)
        z_keep(p).start()
        for k in ctx_steps:
            z_copy(p, k).start()

    def attend(i):
        if groups > 2:
            pl.when(i >= 2)(lambda: spread(i - 2))
        rows = tile(i, PAIR * TOK)
        score = dot_nn(keys_n[...], qct[:, rows]) * SCALE + bias[...]
        expo = jnp.exp(score - jnp.max(score, axis=0, keepdims=True))
        prob = expo * (1.0 / jnp.sum(expo, axis=0, keepdims=True))
        low = prob.astype(BF16)
        pbt[:, rows] = low
        grad = dot_nn(keys_n[:, :D_LAT], glt[:, rows])
        delta = jnp.sum(prob * grad, axis=0, keepdims=True)
        dst[:, rows] = (SCALE * prob * (grad - delta)).astype(BF16)
        keys = gath[...].reshape(WIDTH, n_keys)
        weight_term(i, dot_nn(keys[:D_LAT, :], low).astype(BF16), g, i)

    def query_side(i):
        spread(groups + i - 2)
        rows = tile(i, PAIR * TOK)
        keys = gath[...].reshape(WIDTH, n_keys)
        low = dot_nn(keys, dst[:, rows]).astype(BF16)
        qlt[:, rows] = low
        weight_term(groups + i, low, qn, i)

    own_rows = TOK // n_head

    def key_side(k):
        cols = tile(k, TOK)
        value = dot_nn(pbt[cols, :], gl[...])
        key = dot_nn(dst[cols, :], qc[...])
        low = key[:, :D_LAT] + value
        gsend[:, k, :, :D_LAT] = low.reshape(n_head, own_rows, D_LAT).astype(BF16)
        gsend[:, k, :, D_LAT:] = key[:, D_LAT:].reshape(n_head, own_rows, D_ROPE).astype(BF16)

    each(0, groups, attend)
    each(0, groups, query_side)
    for i in range(2):
        each(i * n_ctx // 2, (i + 1) * n_ctx // 2, key_side)
        spread(pieces - 2 + i)
    h_keep = pltpu.make_async_copy(gsend.at[head], hrecv.at[n_head - 1], hown_s.at[0])
    h_keep.start()
    for k in range(1, n_head):
        h_copy(k).start()

    def nope(i):
        for sub in range(PAIR):
            rows = tile(i * PAIR + sub, 128)
            d_qn[0, :, rows] = dot_tn(qlt[:D_LAT, rows], wk[:, rows]).astype(BF16)

    each(0, groups, nope)
    for m in range(groups * PAIR):
        d_qr[0, :, m * D_ROPE:(m + 1) * D_ROPE] = qlt[D_LAT:, m * TOK:(m + 1) * TOK].T

    def settle(p):
        z_keep(p).wait()
        total = zrecv[p, n_ctx - 1].astype(F32)
        for k in ctx_steps:
            z_copy(p, k).wait_recv()
            total = total + zrecv[p, k - 1].astype(F32)
        own[p] = total.astype(BF16)
        for k in ctx_steps:
            ag_copy(p, k).start()
        yag_copy(p, 0).start()
        own_keep(p).start()

    def hand_on(p):
        for k in ctx_steps:
            there = final.at[p, rep, ctx_at(-k)]
            copy(there, there, ag_s.at[p, k - 1], ag_r.at[p, k - 1],
                 (rep, ctx_at(k), head)).wait_recv()
            yag_copy(p, k).start()

    def latent_terms():
        h_keep.wait()
        for k in range(1, n_head):
            h_copy(k).wait_recv()
        for k in range(n_ctx):
            total = hrecv[n_head - 1, k].astype(F32)
            for i in range(n_head - 1):
                total = total + hrecv[i, k].astype(F32)
            if k == 0:
                d_lat[...] = total
            else:
                lsend[k - 1] = total.astype(BF16)
                l_copy(k).start()

    def settle_next(p):
        settle(p)
        hand_on(p - groups)

    each(0, groups, settle)
    latent_terms()
    each(groups, pieces, settle_next)
    each(groups, pieces, hand_on)
    total = d_lat[...]
    for k in ctx_steps:
        l_copy(k).wait_recv()
        total = total + lrecv[k - 1].astype(F32)
    d_lat[...] = total

    for k in ctx_steps:
        lat_copy(k).wait_send()
        fwd_copy(k).wait_send()
        l_copy(k).wait_send()
    for k in range(1, n_head):
        h_copy(k).wait_send()

    def end(p):
        y_copy(p).wait_send()
        own_keep(p).wait()
        for k in ctx_steps:
            z_copy(p, k).wait_send()
            ag_copy(p, k).wait_send()
        for k in range(n_ctx):
            there = final.at[p, other, ctx_at(-k)]
            arrived = copy(there, there, yag_s.at[p, k], yag_r.at[p, k], (other, ctx, head))
            arrived.wait_recv()
            yag_copy(p, k).wait_send()

    each(0, pieces, end)


def finish(groups, lat, qn, qr, weights, d_lat, d_qn, d_qr, d_wk, d_wv):
    d_lat[0] = lat[...]
    d_qn[...] = qn[...]
    d_qr[...] = qr[...]
    for which, out in ((0, d_wv), (1, d_wk)):
        for i in range(groups):
            value = weights[which * groups + i].reshape(D_LAT, PAIR * 128)
            out[:, i * PAIR * 128:(i + 1) * PAIR * 128] = value.astype(F32)


def local(n_ctx, n_head, latent, q_nope, q_rope, grad_out, w_uk, w_uv, stretch_order):
    heads = w_uk.shape[1] // D_NOPE
    groups = heads // PAIR
    pieces = 2 * groups
    rows = heads * TOK
    n_keys = n_ctx * TOK
    own = TOK // n_head
    part = (D_LAT // (2 * n_ctx), PAIR * 128)
    vmem = pl.BlockSpec(memory_space=pltpu.VMEM)
    anywhere = pl.BlockSpec(memory_space=pl.ANY)
    dma = pltpu.SemaphoreType.DMA
    lat_out, qn_out, qr_out, weights = pl.pallas_call(
        functools.partial(body, n_ctx, n_head, groups),
        out_shape=(
            jax.ShapeDtypeStruct((own, WIDTH), F32),
            jax.ShapeDtypeStruct(q_nope.shape, BF16),
            jax.ShapeDtypeStruct(q_rope.shape, BF16),
            jax.ShapeDtypeStruct((pieces, 2, n_ctx) + part, BF16),
        ),
        in_specs=[anywhere] * 6 + [pl.BlockSpec(memory_space=pltpu.SMEM)],
        out_specs=(vmem,) * 4,
        scratch_shapes=[
            pltpu.VMEM(q_nope.shape, BF16),
            pltpu.VMEM(q_rope.shape, BF16),
            pltpu.VMEM(grad_out.shape, BF16),
            pltpu.VMEM(w_uk.shape, BF16),
            pltpu.VMEM(w_uv.shape, BF16),
            pltpu.VMEM((2, WIDTH // 2, n_keys), BF16),
            pltpu.VMEM((n_keys, WIDTH), BF16),
            pltpu.VMEM((rows, WIDTH), BF16),
            pltpu.VMEM((rows, D_LAT), BF16),
            pltpu.VMEM((WIDTH, rows), BF16),
            pltpu.VMEM((D_LAT, rows), BF16),
            pltpu.VMEM((WIDTH, rows), BF16),
            pltpu.VMEM((n_keys, PAIR * TOK), F32),
            pltpu.VMEM((n_keys, rows), BF16),
            pltpu.VMEM((n_keys, rows), BF16),
            pltpu.VMEM((pieces, 2, n_ctx) + part, BF16),
            pltpu.VMEM((pieces, n_ctx) + part, BF16),
            pltpu.VMEM((pieces, n_ctx) + part, BF16),
            pltpu.VMEM((pieces, n_ctx) + part, BF16),
            pltpu.VMEM((pieces, n_ctx) + part, BF16),
            pltpu.VMEM((pieces,) + part, BF16),
            pltpu.VMEM((n_head, n_ctx, own, WIDTH), BF16),
            pltpu.VMEM((n_head, n_ctx, own, WIDTH), BF16),
            pltpu.VMEM((n_ctx - 1, own, WIDTH), BF16),
            pltpu.VMEM((n_ctx - 1, own, WIDTH), BF16),
            dma((n_ctx - 1,)), dma((n_ctx - 1,)),
            dma((n_ctx - 1,)), dma((n_ctx - 1,)),
            dma((pieces,)), dma((pieces,)),
            dma((pieces, n_ctx - 1)), dma((pieces, n_ctx - 1)),
            dma((pieces, n_ctx - 1)), dma((pieces, n_ctx - 1)),
            dma((pieces, n_ctx)), dma((pieces, n_ctx)),
            dma((n_head - 1,)), dma((n_head - 1,)),
            dma((n_ctx - 1,)), dma((n_ctx - 1,)),
            dma((pieces,)), dma((pieces,)), dma((pieces,)), dma((1,)), dma((6,)),
        ],
        compiler_params=pltpu.CompilerParams(
            collective_id=0, has_side_effects=True, vmem_limit_bytes=56 << 20
        ),
    )(latent.transpose(0, 2, 1).reshape(2, WIDTH // 2, TOK), q_nope, q_rope, grad_out, w_uk, w_uv,
      stretch_order)
    return pl.pallas_call(
        functools.partial(finish, groups),
        out_shape=(
            jax.ShapeDtypeStruct((1, own, WIDTH), F32),
            jax.ShapeDtypeStruct(q_nope.shape, BF16),
            jax.ShapeDtypeStruct(q_rope.shape, BF16),
            jax.ShapeDtypeStruct(w_uk.shape, F32),
            jax.ShapeDtypeStruct(w_uv.shape, F32),
        ),
        in_specs=[vmem] * 4,
        out_specs=(vmem,) * 5,
        compiler_params=pltpu.CompilerParams(vmem_limit_bytes=60 << 20),
    )(lat_out, qn_out, qr_out, weights)


def solution(mesh):
    n_ctx, n_head = mesh.shape["ctx"], mesh.shape["head"]
    placed = (
        P("dp", "ctx", None),
        P("dp", "ctx", "head"),
        P("dp", "ctx", "head"),
        P("dp", "ctx", "head"),
        P(None, "head"),
        P(None, "head"),
        P(),
    )
    return jax.shard_map(
        functools.partial(local, n_ctx, n_head),
        mesh=mesh,
        in_specs=placed,
        out_specs=(
            P("dp", ("ctx", "head"), None),
            P("dp", "ctx", "head"),
            P("dp", "ctx", "head"),
            P(None, "head"),
            P(None, "head"),
        ),
        check_vma=False,
    )
```

```python
import functools
import math

import jax
import jax.numpy as jnp
from jax import lax
from jax.experimental import pallas as pl
from jax.experimental.pallas import tpu as pltpu
from jax.sharding import PartitionSpec as P

D_LAT = 512
D_ROPE = 64
D_NOPE = 128
D_V = 128
TOK = 128
STRETCH = 64
PAIR = 2
WIDTH = D_LAT + D_ROPE
SCALE = 1.0 / math.sqrt(D_NOPE + D_ROPE)
MESH = pl.DeviceIdType.MESH
BF16 = jnp.bfloat16
F32 = jnp.float32


def dot_nn(a, b):
    return jnp.dot(a, b, preferred_element_type=F32)


def dot_nt(a, b):
    return lax.dot_general(a, b, (((1,), (1,)), ((), ())), preferred_element_type=F32)


def dot_tn(a, b):
    return lax.dot_general(a, b, (((0,), (0,)), ((), ())), preferred_element_type=F32)


def body(
    n_ctx, n_head, groups,
    lat, qn_in, qr_in, g_in, wk_in, wv_in, order,
    d_lat, d_qn, d_qr, final,
    qn, qr, g, wk, wv,
    gath, keys_n, qc, gl, qct, glt, qlt, bias, pbt, dst,
    wpart, yown, yrecv, gsend, hrecv, lsend, lrecv,
    lat_s, lat_r, fwd_s, fwd_r, y_s, y_r, z_s, z_r, ag_s, ag_r, yag_s, yag_r, h_s, h_r, l_s, l_r,
    yown_s, hown_s, in_s, *held,
):
    rep = lax.axis_index("dp")
    ctx = lax.axis_index("ctx")
    head = lax.axis_index("head")
    other = 1 - rep
    half = lax.rem(head, 2)
    sibling = head + 1 - 2 * half
    pieces = 2 * groups
    part_rows = wpart.shape[3]
    levels = n_ctx.bit_length() - 1
    held, got = held[:levels], held[levels:]
    bits = [lax.rem(ctx // (1 << v), 2) for v in range(levels)]
    mates = [(rep, ctx + (1 - 2 * bits[v]) * (1 << v), head) for v in range(levels)]
    spans = [n_ctx >> (v + 1) for v in range(levels)]
    begins = [sum(bits[u] * spans[u] for u in range(v + 1)) for v in range(levels)]
    n_keys = n_ctx * TOK
    ctx_steps = range(1, n_ctx)

    def ctx_at(step):
        return lax.rem(ctx + step + n_ctx, n_ctx)

    def head_at(step):
        return lax.rem(head + step + n_head, n_head)

    def copy(src, dst, send, recv, target):
        return pltpu.make_async_remote_copy(
            src_ref=src, dst_ref=dst, send_sem=send, recv_sem=recv,
            device_id=target, device_id_type=MESH,
        )

    def each(first, last, step):
        def run(i, carry):
            step(i)
            return carry

        lax.fori_loop(first, last, run, 0)

    def tile(m, size):
        return pl.ds(pl.multiple_of(m * size, size), size)

    def lat_copy(k):
        cols = slice(k * TOK, (k + 1) * TOK)
        return copy(lat.at[half], gath.at[half, :, cols], lat_s.at[k - 1], lat_r.at[k - 1],
                    (rep, ctx_at(k), head))

    def fwd_copy(k):
        block = gath.at[half, :, slice(k * TOK, (k + 1) * TOK)]
        return copy(block, block, fwd_s.at[k - 1], fwd_r.at[k - 1], (rep, ctx, sibling))

    def y_copy(p):
        return copy(wpart.at[p, other], yrecv.at[p], y_s.at[p], y_r.at[p], (other, ctx, head))

    def y_keep(p):
        return pltpu.make_async_copy(wpart.at[p, rep], yown.at[p], yown_s.at[p])

    def halve_copy(p, v):
        away = held[v].at[p, pl.ds((1 - bits[v]) * spans[v], spans[v])]
        return copy(away, got[v].at[p], z_s.at[p, v], z_r.at[p, v], mates[v])

    def double_copy(p, v):
        mine = final.at[p, rep, pl.ds(begins[v], spans[v])]
        return copy(mine, mine, ag_s.at[p, v], ag_r.at[p, v], mates[v])

    def theirs(p, v, side):
        first = begins[v] + (1 - 2 * bits[v]) * spans[v]
        return final.at[p, side, pl.ds(first, spans[v])]

    def yag_copy(p, v, side):
        if v == levels:
            there = final.at[p, side, pl.ds(begins[levels - 1], 1)]
        else:
            there = theirs(p, v, side)
        return copy(there, there, yag_s.at[p, v], yag_r.at[p, v], (other, ctx, head))

    def h_copy(k):
        return copy(gsend.at[head_at(k)], hrecv.at[k - 1], h_s.at[k - 1], h_r.at[k - 1],
                    (rep, ctx, head_at(k)))

    def l_copy(k):
        return copy(lsend.at[k - 1], lrecv.at[k - 1], l_s.at[k - 1], l_r.at[k - 1],
                    (rep, ctx_at(-k), head))

    fetches = [
        pltpu.make_async_copy(src, dst, in_s.at[i])
        for i, (src, dst) in enumerate((
            (lat, gath.at[:, :, :TOK]), (qn_in, qn), (wk_in, wk), (g_in, g), (wv_in, wv), (qr_in, qr),
        ))
    ]
    for c in fetches:
        c.start()

    partners = [(rep, ctx_at(k), head) for k in ctx_steps]
    partners += [(rep, ctx, head_at(k)) for k in range(1, n_head)]
    partners += [(other, ctx, head)]
    barrier = pltpu.get_barrier_semaphore()
    for target in partners:
        pl.semaphore_signal(barrier, inc=1, device_id=target, device_id_type=MESH)
    pl.semaphore_wait(barrier, len(partners))

    for k in ctx_steps:
        lat_copy(k).start()
    for c in fetches:
        c.wait()

    def project(i):
        for sub in range(PAIR):
            rows = tile(i * PAIR + sub, 128)
            qn_h, g_h, wk_h, wv_h = qn[0, :, rows], g[0, :, rows], wk[:, rows], wv[:, rows]
            qc[rows, :D_LAT] = dot_nt(qn_h, wk_h).astype(BF16)
            gl[rows, :] = dot_nt(g_h, wv_h).astype(BF16)
            qct[:D_LAT, rows] = dot_nt(wk_h, qn_h).astype(BF16)
            glt[:, rows] = dot_nt(wv_h, g_h).astype(BF16)

    each(0, groups, project)
    rope_t = qr[0].T
    for m in range(groups * PAIR):
        rows, cols = slice(m * TOK, (m + 1) * TOK), slice(m * D_ROPE, (m + 1) * D_ROPE)
        qc[rows, D_LAT:] = qr[0, :, cols]
        qct[D_LAT:, rows] = rope_t[cols, :]

    lane = lax.broadcasted_iota(jnp.int32, (1, PAIR * TOK), 1) % TOK
    row_start = jnp.where(lane < STRETCH, order[2 * ctx], order[2 * ctx + 1]) * STRETCH
    row_pos = row_start + lane % STRETCH
    inner = lax.broadcasted_iota(jnp.int32, (STRETCH, PAIR * TOK), 0)
    for k in range(n_ctx):
        owner = ctx_at(-k)
        for part in range(2):
            key_pos = inner + order[2 * owner + part] * STRETCH
            first = k * TOK + part * STRETCH
            bias[first:first + STRETCH, :] = jnp.where(key_pos <= row_pos, 0.0, -jnp.inf)

    def turn(k):
        rows = slice(k * TOK, (k + 1) * TOK)
        keys_n[rows, :] = gath[:, :, rows].reshape(WIDTH, TOK).T

    turn(0)
    for k in ctx_steps:
        lat_copy(k).wait_recv()
        fwd_copy(k).start()
    for k in ctx_steps:
        fwd_copy(k).wait_recv()
        turn(k)

    def weight_term(p, low, value, i):
        for sub in range(PAIR):
            cols = tile(i * PAIR + sub, 128)
            term = dot_nn(low[:D_LAT, sub * TOK:(sub + 1) * TOK], value[0, :, cols]).astype(BF16)
            wpart[p, :, :, :, sub * 128:(sub + 1) * 128] = term.reshape(2, n_ctx, part_rows, 128)
        y_keep(p).start()
        y_copy(p).start()

    def spread(p):
        y_keep(p).wait()
        y_copy(p).wait_recv()

        def add(i):
            total = yown[p, i].astype(F32) + yrecv[p, i].astype(F32)
            held[0][p, i] = total.astype(BF16)

        each(0, n_ctx, add)
        halve_copy(p, 0).start()

    def attend(i):
        if groups > 2:
            pl.when(i >= 2)(lambda: spread(i - 2))
        rows = tile(i, PAIR * TOK)
        score = dot_nn(keys_n[...], qct[:, rows]) * SCALE + bias[...]
        expo = jnp.exp(score - jnp.max(score, axis=0, keepdims=True))
        prob = expo * (1.0 / jnp.sum(expo, axis=0, keepdims=True))
        low = prob.astype(BF16)
        pbt[:, rows] = low
        grad = dot_nn(keys_n[:, :D_LAT], glt[:, rows])
        delta = jnp.sum(prob * grad, axis=0, keepdims=True)
        dst[:, rows] = (SCALE * prob * (grad - delta)).astype(BF16)
        keys = gath[...].reshape(WIDTH, n_keys)
        weight_term(i, dot_nn(keys[:D_LAT, :], low).astype(BF16), g, i)

    def query_side(i):
        spread(groups + i - 2)
        rows = tile(i, PAIR * TOK)
        keys = gath[...].reshape(WIDTH, n_keys)
        low = dot_nn(keys, dst[:, rows]).astype(BF16)
        qlt[:, rows] = low
        weight_term(groups + i, low, qn, i)

    own_rows = TOK // n_head

    def key_side(k):
        cols = tile(k, TOK)
        value = dot_nn(pbt[cols, :], gl[...])
        key = dot_nn(dst[cols, :], qc[...])
        low = key[:, :D_LAT] + value
        gsend[:, k, :, :D_LAT] = low.reshape(n_head, own_rows, D_LAT).astype(BF16)
        gsend[:, k, :, D_LAT:] = key[:, D_LAT:].reshape(n_head, own_rows, D_ROPE).astype(BF16)

    def nope(i):
        for sub in range(PAIR):
            rows = tile(i * PAIR + sub, 128)
            d_qn[0, :, rows] = dot_tn(qlt[:D_LAT, rows], wk[:, rows]).astype(BF16)

    def local_results():
        each(0, groups, nope)
        for m in range(groups * PAIR):
            d_qr[0, :, m * D_ROPE:(m + 1) * D_ROPE] = qlt[D_LAT:, m * TOK:(m + 1) * TOK].T

    def latent_terms():
        h_keep.wait()
        for k in range(1, n_head):
            h_copy(k).wait_recv()
        for k in range(n_ctx):
            total = hrecv[n_head - 1, k].astype(F32)
            for i in range(n_head - 1):
                total = total + hrecv[i, k].astype(F32)
            if k == 0:
                d_lat[...] = total
            else:
                lsend[k - 1] = total.astype(BF16)
                l_copy(k).start()

    h_keep = pltpu.make_async_copy(gsend.at[head], hrecv.at[n_head - 1], hown_s.at[0])

    def send_latent_terms():
        h_keep.start()
        for k in range(1, n_head):
            h_copy(k).start()

    def reduce_step(p, v):
        halve_copy(p, v).wait_recv()

        def add(i):
            total = held[v][p, bits[v] * spans[v] + i].astype(F32) + got[v][p, i].astype(F32)
            if v + 1 < levels:
                held[v + 1][p, i] = total.astype(BF16)
            else:
                final[p, rep, begins[v]] = total.astype(BF16)

        each(0, spans[v], add)
        if v + 1 < levels:
            halve_copy(p, v + 1).start()
        else:
            double_copy(p, v).start()
            yag_copy(p, levels, rep).start()

    def spread_step(p, v):
        there = theirs(p, v, rep)
        copy(there, there, ag_s.at[p, v], ag_r.at[p, v], mates[v]).wait_recv()
        if v > 0:
            double_copy(p, v - 1).start()
        yag_copy(p, v, rep).start()

    done = {(p, 0) for p in range(pieces - 2)}

    def stage(p, at):
        if (p, at) in done:
            return
        done.add((p, at))
        if at == 0:
            spread(p)
        elif at <= levels:
            reduce_step(p, at - 1)
        else:
            spread_step(p, 2 * levels - at)

    each(0, groups, attend)
    each(0, groups, query_side)
    stage(0, 1)
    stage(pieces - 2, 0)
    stage(1, 1)
    each(0, n_ctx // 2, key_side)
    stage(0, 2)
    stage(pieces - 1, 0)
    stage(2, 1)
    stage(1, 2)
    each(n_ctx // 2, n_ctx, key_side)
    send_latent_terms()
    for wave in range(2 * levels + pieces):
        for p in range(pieces):
            if 0 <= wave - p <= 2 * levels:
                stage(p, wave - p)
        if wave == pieces:
            local_results()
            latent_terms()
    total = d_lat[...]
    for k in ctx_steps:
        l_copy(k).wait_recv()
        total = total + lrecv[k - 1].astype(F32)
    d_lat[...] = total

    for k in ctx_steps:
        lat_copy(k).wait_send()
        fwd_copy(k).wait_send()
        l_copy(k).wait_send()
    for k in range(1, n_head):
        h_copy(k).wait_send()

    def end(p):
        y_copy(p).wait_send()
        for v in range(levels):
            halve_copy(p, v).wait_send()
            double_copy(p, v).wait_send()
        for v in range(levels + 1):
            yag_copy(p, v, other).wait_recv()
            yag_copy(p, v, rep).wait_send()

    each(0, pieces, end)


def finish(groups, lat, qn, qr, weights, d_lat, d_qn, d_qr, d_wk, d_wv):
    d_lat[0] = lat[...]
    d_qn[...] = qn[...]
    d_qr[...] = qr[...]
    for which, out in ((0, d_wv), (1, d_wk)):
        for i in range(groups):
            value = weights[which * groups + i].reshape(D_LAT, PAIR * 128)
            out[:, i * PAIR * 128:(i + 1) * PAIR * 128] = value.astype(F32)


def local(n_ctx, n_head, latent, q_nope, q_rope, grad_out, w_uk, w_uv, stretch_order):
    heads = w_uk.shape[1] // D_NOPE
    groups = heads // PAIR
    pieces = 2 * groups
    rows = heads * TOK
    n_keys = n_ctx * TOK
    own = TOK // n_head
    levels = n_ctx.bit_length() - 1
    part = (D_LAT // (2 * n_ctx), PAIR * 128)
    vmem = pl.BlockSpec(memory_space=pltpu.VMEM)
    anywhere = pl.BlockSpec(memory_space=pl.ANY)
    dma = pltpu.SemaphoreType.DMA
    lat_out, qn_out, qr_out, weights = pl.pallas_call(
        functools.partial(body, n_ctx, n_head, groups),
        out_shape=(
            jax.ShapeDtypeStruct((own, WIDTH), F32),
            jax.ShapeDtypeStruct(q_nope.shape, BF16),
            jax.ShapeDtypeStruct(q_rope.shape, BF16),
            jax.ShapeDtypeStruct((pieces, 2, n_ctx) + part, BF16),
        ),
        in_specs=[anywhere] * 6 + [pl.BlockSpec(memory_space=pltpu.SMEM)],
        out_specs=(vmem,) * 4,
        scratch_shapes=[
            pltpu.VMEM(q_nope.shape, BF16),
            pltpu.VMEM(q_rope.shape, BF16),
            pltpu.VMEM(grad_out.shape, BF16),
            pltpu.VMEM(w_uk.shape, BF16),
            pltpu.VMEM(w_uv.shape, BF16),
            pltpu.VMEM((2, WIDTH // 2, n_keys), BF16),
            pltpu.VMEM((n_keys, WIDTH), BF16),
            pltpu.VMEM((rows, WIDTH), BF16),
            pltpu.VMEM((rows, D_LAT), BF16),
            pltpu.VMEM((WIDTH, rows), BF16),
            pltpu.VMEM((D_LAT, rows), BF16),
            pltpu.VMEM((WIDTH, rows), BF16),
            pltpu.VMEM((n_keys, PAIR * TOK), F32),
            pltpu.VMEM((n_keys, rows), BF16),
            pltpu.VMEM((n_keys, rows), BF16),
            pltpu.VMEM((pieces, 2, n_ctx) + part, BF16),
            pltpu.VMEM((pieces, n_ctx) + part, BF16),
            pltpu.VMEM((pieces, n_ctx) + part, BF16),
            pltpu.VMEM((n_head, n_ctx, own, WIDTH), BF16),
            pltpu.VMEM((n_head, n_ctx, own, WIDTH), BF16),
            pltpu.VMEM((n_ctx - 1, own, WIDTH), BF16),
            pltpu.VMEM((n_ctx - 1, own, WIDTH), BF16),
            dma((n_ctx - 1,)), dma((n_ctx - 1,)),
            dma((n_ctx - 1,)), dma((n_ctx - 1,)),
            dma((pieces,)), dma((pieces,)),
            dma((pieces, levels)), dma((pieces, levels)),
            dma((pieces, levels)), dma((pieces, levels)),
            dma((pieces, levels + 1)), dma((pieces, levels + 1)),
            dma((n_head - 1,)), dma((n_head - 1,)),
            dma((n_ctx - 1,)), dma((n_ctx - 1,)),
            dma((pieces,)), dma((1,)), dma((6,)),
        ]
        + [pltpu.VMEM((pieces, n_ctx >> v) + part, BF16) for v in range(levels)]
        + [pltpu.VMEM((pieces, n_ctx >> (v + 1)) + part, BF16) for v in range(levels)],
        compiler_params=pltpu.CompilerParams(
            collective_id=0, has_side_effects=True, vmem_limit_bytes=56 << 20
        ),
    )(latent.transpose(0, 2, 1).reshape(2, WIDTH // 2, TOK), q_nope, q_rope, grad_out, w_uk, w_uv,
      stretch_order)
    return pl.pallas_call(
        functools.partial(finish, groups),
        out_shape=(
            jax.ShapeDtypeStruct((1, own, WIDTH), F32),
            jax.ShapeDtypeStruct(q_nope.shape, BF16),
            jax.ShapeDtypeStruct(q_rope.shape, BF16),
            jax.ShapeDtypeStruct(w_uk.shape, F32),
            jax.ShapeDtypeStruct(w_uv.shape, F32),
        ),
        in_specs=[vmem] * 4,
        out_specs=(vmem,) * 5,
        compiler_params=pltpu.CompilerParams(vmem_limit_bytes=60 << 20),
    )(lat_out, qn_out, qr_out, weights)


def solution(mesh):
    n_ctx, n_head = mesh.shape["ctx"], mesh.shape["head"]
    placed = (
        P("dp", "ctx", None),
        P("dp", "ctx", "head"),
        P("dp", "ctx", "head"),
        P("dp", "ctx", "head"),
        P(None, "head"),
        P(None, "head"),
        P(),
    )
    return jax.shard_map(
        functools.partial(local, n_ctx, n_head),
        mesh=mesh,
        in_specs=placed,
        out_specs=(
            P("dp", ("ctx", "head"), None),
            P("dp", "ctx", "head"),
            P("dp", "ctx", "head"),
            P(None, "head"),
            P(None, "head"),
        ),
        check_vma=False,
    )
```

```python
import functools
import math

import jax
import jax.numpy as jnp
from jax import lax
from jax.experimental import pallas as pl
from jax.experimental.pallas import tpu as pltpu
from jax.sharding import PartitionSpec as P

D_LAT = 512
D_ROPE = 64
D_NOPE = 128
D_V = 128
TOK = 128
STRETCH = 64
PAIR = 2
WIDTH = D_LAT + D_ROPE
SCALE = 1.0 / math.sqrt(D_NOPE + D_ROPE)
MESH = pl.DeviceIdType.MESH
BF16 = jnp.bfloat16
F32 = jnp.float32


def dot_nn(a, b):
    return jnp.dot(a, b, preferred_element_type=F32)


def dot_nt(a, b):
    return lax.dot_general(a, b, (((1,), (1,)), ((), ())), preferred_element_type=F32)


def dot_tn(a, b):
    return lax.dot_general(a, b, (((0,), (0,)), ((), ())), preferred_element_type=F32)


def body(
    n_ctx, n_head, groups,
    lat, qn_in, qr_in, g_in, wk_in, wv_in, order,
    d_lat, d_qn, d_qr, final,
    qn, qr, g, wk, wv,
    gath, keys_n, qc, gl, qct, glt, qlt, bias, pbt, dst,
    wpart, yown, yrecv, gsend, hrecv, lsend, lrecv,
    lat_s, lat_r, fwd_s, fwd_r, y_s, y_r, z_s, z_r, ag_s, ag_r, yag_s, yag_r, h_s, h_r, l_s, l_r,
    yown_s, hown_s, in_s, *held,
):
    rep = lax.axis_index("dp")
    ctx = lax.axis_index("ctx")
    head = lax.axis_index("head")
    other = 1 - rep
    half = lax.rem(head, 2)
    sibling = head + 1 - 2 * half
    pieces = 2 * groups
    part_rows = wpart.shape[3]
    levels = n_ctx.bit_length() - 1
    wide = groups
    held, got = held[:levels], held[levels:]
    bits = [lax.rem(ctx // (1 << v), 2) for v in range(levels)]
    mates = [(rep, ctx + (1 - 2 * bits[v]) * (1 << v), head) for v in range(levels)]
    spans = [n_ctx >> (v + 1) for v in range(levels)]
    begins = [sum(bits[u] * spans[u] for u in range(v + 1)) for v in range(levels)]
    n_keys = n_ctx * TOK
    ctx_steps = range(1, n_ctx)

    def ctx_at(step):
        return lax.rem(ctx + step + n_ctx, n_ctx)

    def head_at(step):
        return lax.rem(head + step + n_head, n_head)

    def copy(src, dst, send, recv, target):
        return pltpu.make_async_remote_copy(
            src_ref=src, dst_ref=dst, send_sem=send, recv_sem=recv,
            device_id=target, device_id_type=MESH,
        )

    def each(first, last, step):
        def run(i, carry):
            step(i)
            return carry

        lax.fori_loop(first, last, run, 0)

    def tile(m, size):
        return pl.ds(pl.multiple_of(m * size, size), size)

    def lat_copy(k):
        cols = slice(k * TOK, (k + 1) * TOK)
        return copy(lat.at[half], gath.at[half, :, cols], lat_s.at[k - 1], lat_r.at[k - 1],
                    (rep, ctx_at(k), head))

    def fwd_copy(k):
        block = gath.at[half, :, slice(k * TOK, (k + 1) * TOK)]
        return copy(block, block, fwd_s.at[k - 1], fwd_r.at[k - 1], (rep, ctx, sibling))

    def y_copy(p):
        return copy(wpart.at[p, other], yrecv.at[p], y_s.at[p], y_r.at[p], (other, ctx, head))

    def y_keep(p):
        return pltpu.make_async_copy(wpart.at[p, rep], yown.at[p], yown_s.at[p])

    def halve_copy(p, v):
        away = held[v].at[p, pl.ds((1 - bits[v]) * spans[v], spans[v])]
        return copy(away, got[v].at[p], z_s.at[p, v], z_r.at[p, v], mates[v])

    def double_copy(p, v):
        sides = slice(0, 2) if p < wide else rep
        mine = final.at[p, sides, pl.ds(begins[v], spans[v])]
        return copy(mine, mine, ag_s.at[p, v], ag_r.at[p, v], mates[v])

    def theirs(p, v, side):
        first = begins[v] + (1 - 2 * bits[v]) * spans[v]
        return final.at[p, side, pl.ds(first, spans[v])]

    def yag_copy(p, v, side):
        if v == levels:
            there = final.at[p, side, pl.ds(begins[levels - 1], 1)]
        else:
            there = theirs(p, v, side)
        return copy(there, there, yag_s.at[p, v], yag_r.at[p, v], (other, ctx, head))

    def h_copy(k):
        return copy(gsend.at[head_at(k)], hrecv.at[k - 1], h_s.at[k - 1], h_r.at[k - 1],
                    (rep, ctx, head_at(k)))

    def l_copy(k):
        return copy(lsend.at[k - 1], lrecv.at[k - 1], l_s.at[k - 1], l_r.at[k - 1],
                    (rep, ctx_at(-k), head))

    fetches = [
        pltpu.make_async_copy(src, dst, in_s.at[i])
        for i, (src, dst) in enumerate((
            (lat, gath.at[:, :, :TOK]), (qn_in, qn), (wk_in, wk), (g_in, g), (wv_in, wv), (qr_in, qr),
        ))
    ]
    for c in fetches:
        c.start()

    partners = [(rep, ctx_at(k), head) for k in ctx_steps]
    partners += [(rep, ctx, head_at(k)) for k in range(1, n_head)]
    partners += [(other, ctx, head)]
    barrier = pltpu.get_barrier_semaphore()
    for target in partners:
        pl.semaphore_signal(barrier, inc=1, device_id=target, device_id_type=MESH)
    pl.semaphore_wait(barrier, len(partners))

    for k in ctx_steps:
        lat_copy(k).start()
    for c in fetches:
        c.wait()

    def project(i):
        for sub in range(PAIR):
            rows = tile(i * PAIR + sub, 128)
            qn_h, g_h, wk_h, wv_h = qn[0, :, rows], g[0, :, rows], wk[:, rows], wv[:, rows]
            qc[rows, :D_LAT] = dot_nt(qn_h, wk_h).astype(BF16)
            gl[rows, :] = dot_nt(g_h, wv_h).astype(BF16)
            qct[:D_LAT, rows] = dot_nt(wk_h, qn_h).astype(BF16)
            glt[:, rows] = dot_nt(wv_h, g_h).astype(BF16)

    each(0, groups, project)
    rope_t = qr[0].T
    for m in range(groups * PAIR):
        rows, cols = slice(m * TOK, (m + 1) * TOK), slice(m * D_ROPE, (m + 1) * D_ROPE)
        qc[rows, D_LAT:] = qr[0, :, cols]
        qct[D_LAT:, rows] = rope_t[cols, :]

    lane = lax.broadcasted_iota(jnp.int32, (1, PAIR * TOK), 1) % TOK
    row_start = jnp.where(lane < STRETCH, order[2 * ctx], order[2 * ctx + 1]) * STRETCH
    row_pos = row_start + lane % STRETCH
    inner = lax.broadcasted_iota(jnp.int32, (STRETCH, PAIR * TOK), 0)
    for k in range(n_ctx):
        owner = ctx_at(-k)
        for part in range(2):
            key_pos = inner + order[2 * owner + part] * STRETCH
            first = k * TOK + part * STRETCH
            bias[first:first + STRETCH, :] = jnp.where(key_pos <= row_pos, 0.0, -jnp.inf)

    def turn(k):
        rows = slice(k * TOK, (k + 1) * TOK)
        keys_n[rows, :] = gath[:, :, rows].reshape(WIDTH, TOK).T

    turn(0)
    for k in ctx_steps:
        lat_copy(k).wait_recv()
        fwd_copy(k).start()
    for k in ctx_steps:
        fwd_copy(k).wait_recv()
        turn(k)

    def weight_term(p, low, value, i):
        for sub in range(PAIR):
            cols = tile(i * PAIR + sub, 128)
            term = dot_nn(low[:D_LAT, sub * TOK:(sub + 1) * TOK], value[0, :, cols]).astype(BF16)
            wpart[p, :, :, :, sub * 128:(sub + 1) * 128] = term.reshape(2, n_ctx, part_rows, 128)
        y_keep(p).start()
        y_copy(p).start()

    def spread(p):
        y_keep(p).wait()
        y_copy(p).wait_recv()

        def add(i):
            total = yown[p, i].astype(F32) + yrecv[p, i].astype(F32)
            held[0][p, i] = total.astype(BF16)

        each(0, n_ctx, add)
        halve_copy(p, 0).start()

    def attend(i):
        if groups > 2:
            pl.when(i >= 2)(lambda: spread(i - 2))
        rows = tile(i, PAIR * TOK)
        score = dot_nn(keys_n[...], qct[:, rows]) * SCALE + bias[...]
        expo = jnp.exp(score - jnp.max(score, axis=0, keepdims=True))
        prob = expo * (1.0 / jnp.sum(expo, axis=0, keepdims=True))
        low = prob.astype(BF16)
        pbt[:, rows] = low
        grad = dot_nn(keys_n[:, :D_LAT], glt[:, rows])
        delta = jnp.sum(prob * grad, axis=0, keepdims=True)
        dst[:, rows] = (SCALE * prob * (grad - delta)).astype(BF16)
        keys = gath[...].reshape(WIDTH, n_keys)
        weight_term(i, dot_nn(keys[:D_LAT, :], low).astype(BF16), g, i)

    def query_side(i):
        spread(groups + i - 2)
        rows = tile(i, PAIR * TOK)
        keys = gath[...].reshape(WIDTH, n_keys)
        low = dot_nn(keys, dst[:, rows]).astype(BF16)
        qlt[:, rows] = low
        weight_term(groups + i, low, qn, i)

    own_rows = TOK // n_head

    def key_side(k):
        cols = tile(k, TOK)
        value = dot_nn(pbt[cols, :], gl[...])
        key = dot_nn(dst[cols, :], qc[...])
        low = key[:, :D_LAT] + value
        gsend[:, k, :, :D_LAT] = low.reshape(n_head, own_rows, D_LAT).astype(BF16)
        gsend[:, k, :, D_LAT:] = key[:, D_LAT:].reshape(n_head, own_rows, D_ROPE).astype(BF16)

    def nope(i):
        for sub in range(PAIR):
            rows = tile(i * PAIR + sub, 128)
            d_qn[0, :, rows] = dot_tn(qlt[:D_LAT, rows], wk[:, rows]).astype(BF16)

    def local_results():
        each(0, groups, nope)
        for m in range(groups * PAIR):
            d_qr[0, :, m * D_ROPE:(m + 1) * D_ROPE] = qlt[D_LAT:, m * TOK:(m + 1) * TOK].T

    def latent_terms():
        h_keep.wait()
        for k in range(1, n_head):
            h_copy(k).wait_recv()
        for k in range(n_ctx):
            total = hrecv[n_head - 1, k].astype(F32)
            for i in range(n_head - 1):
                total = total + hrecv[i, k].astype(F32)
            if k == 0:
                d_lat[...] = total
            else:
                lsend[k - 1] = total.astype(BF16)
                l_copy(k).start()

    h_keep = pltpu.make_async_copy(gsend.at[head], hrecv.at[n_head - 1], hown_s.at[0])

    def send_latent_terms():
        h_keep.start()
        for k in range(1, n_head):
            h_copy(k).start()

    def reduce_step(p, v):
        halve_copy(p, v).wait_recv()

        def add(i):
            total = held[v][p, bits[v] * spans[v] + i].astype(F32) + got[v][p, i].astype(F32)
            if v + 1 < levels:
                held[v + 1][p, i] = total.astype(BF16)
            else:
                final[p, rep, begins[v]] = total.astype(BF16)

        each(0, spans[v], add)
        if v + 1 < levels:
            halve_copy(p, v + 1).start()
        else:
            yag_copy(p, levels, rep).start()
            if p >= wide:
                double_copy(p, v).start()

    def cross_step(p):
        if p < wide:
            yag_copy(p, levels, other).wait_recv()
            double_copy(p, levels - 1).start()

    def spread_step(p, v):
        there = theirs(p, v, slice(0, 2) if p < wide else rep)
        copy(there, there, ag_s.at[p, v], ag_r.at[p, v], mates[v]).wait_recv()
        if v > 0:
            double_copy(p, v - 1).start()
        if p >= wide:
            yag_copy(p, v, rep).start()

    done = {(p, 0) for p in range(pieces - 2)}

    def stage(p, at):
        if (p, at) in done:
            return
        done.add((p, at))
        if at == 0:
            spread(p)
        elif at <= levels:
            reduce_step(p, at - 1)
        elif at == levels + 1:
            cross_step(p)
        else:
            spread_step(p, 2 * levels + 1 - at)

    each(0, groups, attend)
    each(0, groups, query_side)
    stage(0, 1)
    stage(pieces - 2, 0)
    stage(1, 1)
    each(0, n_ctx // 2, key_side)
    stage(0, 2)
    stage(pieces - 1, 0)
    stage(2, 1)
    stage(1, 2)
    each(n_ctx // 2, n_ctx, key_side)
    send_latent_terms()
    for wave in range(2 * levels + 1 + pieces):
        for p in range(pieces):
            if 0 <= wave - p <= 2 * levels + 1:
                stage(p, wave - p)
        if wave == pieces:
            local_results()
            latent_terms()
    total = d_lat[...]
    for k in ctx_steps:
        l_copy(k).wait_recv()
        total = total + lrecv[k - 1].astype(F32)
    d_lat[...] = total

    for k in ctx_steps:
        lat_copy(k).wait_send()
        fwd_copy(k).wait_send()
        l_copy(k).wait_send()
    for k in range(1, n_head):
        h_copy(k).wait_send()

    def end(p):
        y_copy(p).wait_send()
        for v in range(levels):
            halve_copy(p, v).wait_send()
            double_copy(p, v).wait_send()
        yag_copy(p, levels, rep).wait_send()
        if p >= wide:
            yag_copy(p, levels, other).wait_recv()
            for v in range(levels):
                yag_copy(p, v, other).wait_recv()
                yag_copy(p, v, rep).wait_send()

    for p in range(pieces):
        end(p)


def finish(groups, lat, qn, qr, weights, d_lat, d_qn, d_qr, d_wk, d_wv):
    d_lat[0] = lat[...]
    d_qn[...] = qn[...]
    d_qr[...] = qr[...]
    for which, out in ((0, d_wv), (1, d_wk)):
        for i in range(groups):
            value = weights[which * groups + i].reshape(D_LAT, PAIR * 128)
            out[:, i * PAIR * 128:(i + 1) * PAIR * 128] = value.astype(F32)


def local(n_ctx, n_head, latent, q_nope, q_rope, grad_out, w_uk, w_uv, stretch_order):
    heads = w_uk.shape[1] // D_NOPE
    groups = heads // PAIR
    pieces = 2 * groups
    rows = heads * TOK
    n_keys = n_ctx * TOK
    own = TOK // n_head
    levels = n_ctx.bit_length() - 1
    part = (D_LAT // (2 * n_ctx), PAIR * 128)
    vmem = pl.BlockSpec(memory_space=pltpu.VMEM)
    anywhere = pl.BlockSpec(memory_space=pl.ANY)
    dma = pltpu.SemaphoreType.DMA
    lat_out, qn_out, qr_out, weights = pl.pallas_call(
        functools.partial(body, n_ctx, n_head, groups),
        out_shape=(
            jax.ShapeDtypeStruct((own, WIDTH), F32),
            jax.ShapeDtypeStruct(q_nope.shape, BF16),
            jax.ShapeDtypeStruct(q_rope.shape, BF16),
            jax.ShapeDtypeStruct((pieces, 2, n_ctx) + part, BF16),
        ),
        in_specs=[anywhere] * 6 + [pl.BlockSpec(memory_space=pltpu.SMEM)],
        out_specs=(vmem,) * 4,
        scratch_shapes=[
            pltpu.VMEM(q_nope.shape, BF16),
            pltpu.VMEM(q_rope.shape, BF16),
            pltpu.VMEM(grad_out.shape, BF16),
            pltpu.VMEM(w_uk.shape, BF16),
            pltpu.VMEM(w_uv.shape, BF16),
            pltpu.VMEM((2, WIDTH // 2, n_keys), BF16),
            pltpu.VMEM((n_keys, WIDTH), BF16),
            pltpu.VMEM((rows, WIDTH), BF16),
            pltpu.VMEM((rows, D_LAT), BF16),
            pltpu.VMEM((WIDTH, rows), BF16),
            pltpu.VMEM((D_LAT, rows), BF16),
            pltpu.VMEM((WIDTH, rows), BF16),
            pltpu.VMEM((n_keys, PAIR * TOK), F32),
            pltpu.VMEM((n_keys, rows), BF16),
            pltpu.VMEM((n_keys, rows), BF16),
            pltpu.VMEM((pieces, 2, n_ctx) + part, BF16),
            pltpu.VMEM((pieces, n_ctx) + part, BF16),
            pltpu.VMEM((pieces, n_ctx) + part, BF16),
            pltpu.VMEM((n_head, n_ctx, own, WIDTH), BF16),
            pltpu.VMEM((n_head, n_ctx, own, WIDTH), BF16),
            pltpu.VMEM((n_ctx - 1, own, WIDTH), BF16),
            pltpu.VMEM((n_ctx - 1, own, WIDTH), BF16),
            dma((n_ctx - 1,)), dma((n_ctx - 1,)),
            dma((n_ctx - 1,)), dma((n_ctx - 1,)),
            dma((pieces,)), dma((pieces,)),
            dma((pieces, levels)), dma((pieces, levels)),
            dma((pieces, levels)), dma((pieces, levels)),
            dma((pieces, levels + 1)), dma((pieces, levels + 1)),
            dma((n_head - 1,)), dma((n_head - 1,)),
            dma((n_ctx - 1,)), dma((n_ctx - 1,)),
            dma((pieces,)), dma((1,)), dma((6,)),
        ]
        + [pltpu.VMEM((pieces, n_ctx >> v) + part, BF16) for v in range(levels)]
        + [pltpu.VMEM((pieces, n_ctx >> (v + 1)) + part, BF16) for v in range(levels)],
        compiler_params=pltpu.CompilerParams(
            collective_id=0, has_side_effects=True, vmem_limit_bytes=56 << 20
        ),
    )(latent.transpose(0, 2, 1).reshape(2, WIDTH // 2, TOK), q_nope, q_rope, grad_out, w_uk, w_uv,
      stretch_order)
    return pl.pallas_call(
        functools.partial(finish, groups),
        out_shape=(
            jax.ShapeDtypeStruct((1, own, WIDTH), F32),
            jax.ShapeDtypeStruct(q_nope.shape, BF16),
            jax.ShapeDtypeStruct(q_rope.shape, BF16),
            jax.ShapeDtypeStruct(w_uk.shape, F32),
            jax.ShapeDtypeStruct(w_uv.shape, F32),
        ),
        in_specs=[vmem] * 4,
        out_specs=(vmem,) * 5,
        compiler_params=pltpu.CompilerParams(vmem_limit_bytes=60 << 20),
    )(lat_out, qn_out, qr_out, weights)


def solution(mesh):
    n_ctx, n_head = mesh.shape["ctx"], mesh.shape["head"]
    placed = (
        P("dp", "ctx", None),
        P("dp", "ctx", "head"),
        P("dp", "ctx", "head"),
        P("dp", "ctx", "head"),
        P(None, "head"),
        P(None, "head"),
        P(),
    )
    return jax.shard_map(
        functools.partial(local, n_ctx, n_head),
        mesh=mesh,
        in_specs=placed,
        out_specs=(
            P("dp", ("ctx", "head"), None),
            P("dp", "ctx", "head"),
            P("dp", "ctx", "head"),
            P(None, "head"),
            P(None, "head"),
        ),
        check_vma=False,
    )
```

```python
import functools
import math

import jax
import jax.numpy as jnp
from jax import lax
from jax.experimental import pallas as pl
from jax.experimental.pallas import tpu as pltpu
from jax.sharding import PartitionSpec as P

D_LAT = 512
D_ROPE = 64
D_NOPE = 128
D_V = 128
TOK = 128
STRETCH = 64
PAIR = 2
WIDTH = D_LAT + D_ROPE
SCALE = 1.0 / math.sqrt(D_NOPE + D_ROPE)
MESH = pl.DeviceIdType.MESH
BF16 = jnp.bfloat16
F32 = jnp.float32


def dot_nn(a, b):
    return jnp.dot(a, b, preferred_element_type=F32)


def dot_nt(a, b):
    return lax.dot_general(a, b, (((1,), (1,)), ((), ())), preferred_element_type=F32)


def dot_tn(a, b):
    return lax.dot_general(a, b, (((0,), (0,)), ((), ())), preferred_element_type=F32)


def body(
    n_ctx, n_head, groups,
    lat, qn_in, qr_in, g_in, wk_in, wv_in, order,
    d_lat, d_qn, d_qr, final,
    qn, qr, g, wk, wv,
    gath, keys_n, qc, gl, qct, glt, qlt, bias, pbt, dst,
    wpart, yown, yrecv, zsend, zrecv, own, gsend, hrecv, lsend, lrecv,
    lat_s, lat_r, fwd_s, fwd_r, y_s, y_r, z_s, z_r, ag_s, ag_r, yag_s, yag_r, h_s, h_r, l_s, l_r,
    yown_s, zown_s, own_s, hown_s, in_s,
):
    rep = lax.axis_index("dp")
    ctx = lax.axis_index("ctx")
    head = lax.axis_index("head")
    other = 1 - rep
    half = lax.rem(head, 2)
    sibling = head + 1 - 2 * half
    pieces = 2 * groups
    part_rows = own.shape[1]
    n_keys = n_ctx * TOK
    ctx_steps = range(1, n_ctx)

    def ctx_at(step):
        return lax.rem(ctx + step + n_ctx, n_ctx)

    def head_at(step):
        return lax.rem(head + step + n_head, n_head)

    def copy(src, dst, send, recv, target):
        return pltpu.make_async_remote_copy(
            src_ref=src, dst_ref=dst, send_sem=send, recv_sem=recv,
            device_id=target, device_id_type=MESH,
        )

    def each(first, last, step):
        def run(i, carry):
            step(i)
            return carry

        lax.fori_loop(first, last, run, 0)

    def tile(m, size):
        return pl.ds(pl.multiple_of(m * size, size), size)

    def lat_copy(k):
        cols = slice(k * TOK, (k + 1) * TOK)
        return copy(lat.at[half], gath.at[half, :, cols], lat_s.at[k - 1], lat_r.at[k - 1],
                    (rep, ctx_at(k), head))

    def fwd_copy(k):
        block = gath.at[half, :, slice(k * TOK, (k + 1) * TOK)]
        return copy(block, block, fwd_s.at[k - 1], fwd_r.at[k - 1], (rep, ctx, sibling))

    def y_copy(p):
        return copy(wpart.at[p, other], yrecv.at[p], y_s.at[p], y_r.at[p], (other, ctx, head))

    def y_keep(p):
        return pltpu.make_async_copy(wpart.at[p, rep], yown.at[p], yown_s.at[p])

    def z_copy(p, k):
        return copy(zsend.at[p, ctx_at(k)], zrecv.at[p, k - 1], z_s.at[p, k - 1], z_r.at[p, k - 1],
                    (rep, ctx_at(k), head))

    def z_keep(p):
        return pltpu.make_async_copy(zsend.at[p, ctx], zrecv.at[p, n_ctx - 1], zown_s.at[p])

    def ag_copy(p, k):
        return copy(own.at[p], final.at[p, rep, ctx], ag_s.at[p, k - 1], ag_r.at[p, k - 1],
                    (rep, ctx_at(k), head))

    def own_keep(p):
        return pltpu.make_async_copy(own.at[p], final.at[p, rep, ctx], own_s.at[p])

    def yag_copy(p, k):
        there = final.at[p, rep, ctx_at(-k)]
        return copy(own.at[p] if k == 0 else there, there, yag_s.at[p, k], yag_r.at[p, k],
                    (other, ctx, head))

    def h_copy(k):
        return copy(gsend.at[head_at(k)], hrecv.at[k - 1], h_s.at[k - 1], h_r.at[k - 1],
                    (rep, ctx, head_at(k)))

    def l_copy(k):
        return copy(lsend.at[k - 1], lrecv.at[k - 1], l_s.at[k - 1], l_r.at[k - 1],
                    (rep, ctx_at(-k), head))

    fetches = [
        pltpu.make_async_copy(src, dst, in_s.at[i])
        for i, (src, dst) in enumerate((
            (lat, gath.at[:, :, :TOK]), (qn_in, qn), (wk_in, wk), (g_in, g), (wv_in, wv), (qr_in, qr),
        ))
    ]
    for c in fetches:
        c.start()

    partners = [(rep, ctx_at(k), head) for k in ctx_steps]
    partners += [(rep, ctx, head_at(k)) for k in range(1, n_head)]
    partners += [(other, ctx, head)]
    barrier = pltpu.get_barrier_semaphore()
    for target in partners:
        pl.semaphore_signal(barrier, inc=1, device_id=target, device_id_type=MESH)
    pl.semaphore_wait(barrier, len(partners))

    for k in ctx_steps:
        lat_copy(k).start()
    for c in fetches:
        c.wait()

    def project(i):
        for sub in range(PAIR):
            rows = tile(i * PAIR + sub, 128)
            qn_h, g_h, wk_h, wv_h = qn[0, :, rows], g[0, :, rows], wk[:, rows], wv[:, rows]
            qc[rows, :D_LAT] = dot_nt(qn_h, wk_h).astype(BF16)
            gl[rows, :] = dot_nt(g_h, wv_h).astype(BF16)
            qct[:D_LAT, rows] = dot_nt(wk_h, qn_h).astype(BF16)
            glt[:, rows] = dot_nt(wv_h, g_h).astype(BF16)

    each(0, groups, project)
    rope_t = qr[0].T
    for m in range(groups * PAIR):
        rows, cols = slice(m * TOK, (m + 1) * TOK), slice(m * D_ROPE, (m + 1) * D_ROPE)
        qc[rows, D_LAT:] = qr[0, :, cols]
        qct[D_LAT:, rows] = rope_t[cols, :]

    lane = lax.broadcasted_iota(jnp.int32, (1, PAIR * TOK), 1) % TOK
    row_start = jnp.where(lane < STRETCH, order[2 * ctx], order[2 * ctx + 1]) * STRETCH
    row_pos = row_start + lane % STRETCH
    inner = lax.broadcasted_iota(jnp.int32, (STRETCH, PAIR * TOK), 0)
    for k in range(n_ctx):
        owner = ctx_at(-k)
        for part in range(2):
            key_pos = inner + order[2 * owner + part] * STRETCH
            first = k * TOK + part * STRETCH
            bias[first:first + STRETCH, :] = jnp.where(key_pos <= row_pos, 0.0, -jnp.inf)

    def turn(k):
        rows = slice(k * TOK, (k + 1) * TOK)
        keys_n[rows, :] = gath[:, :, rows].reshape(WIDTH, TOK).T

    turn(0)
    for k in ctx_steps:
        lat_copy(k).wait_recv()
        fwd_copy(k).start()
    for k in ctx_steps:
        fwd_copy(k).wait_recv()
        turn(k)

    def weight_term(p, low, value, i):
        for sub in range(PAIR):
            cols = tile(i * PAIR + sub, 128)
            term = dot_nn(low[:D_LAT, sub * TOK:(sub + 1) * TOK], value[0, :, cols]).astype(BF16)
            wpart[p, :, :, :, sub * 128:(sub + 1) * 128] = term.reshape(2, n_ctx, part_rows, 128)
        y_keep(p).start()
        y_copy(p).start()

    def spread(p):
        y_keep(p).wait()
        y_copy(p).wait_recv()

        def add(i):
            total = yown[p, i].astype(F32) + yrecv[p, i].astype(F32)
            zsend[p, i] = total.astype(BF16)

        each(0, n_ctx, add)
        z_keep(p).start()
        for k in ctx_steps:
            z_copy(p, k).start()

    def attend(i):
        if groups > 2:
            pl.when(i >= 2)(lambda: spread(i - 2))
        rows = tile(i, PAIR * TOK)
        score = dot_nn(keys_n[...], qct[:, rows]) * SCALE + bias[...]
        expo = jnp.exp(score - jnp.max(score, axis=0, keepdims=True))
        prob = expo * (1.0 / jnp.sum(expo, axis=0, keepdims=True))
        low = prob.astype(BF16)
        pbt[:, rows] = low
        grad = dot_nn(keys_n[:, :D_LAT], glt[:, rows])
        delta = jnp.sum(prob * grad, axis=0, keepdims=True)
        dst[:, rows] = (SCALE * prob * (grad - delta)).astype(BF16)
        keys = gath[...].reshape(WIDTH, n_keys)
        weight_term(i, dot_nn(keys[:D_LAT, :], low).astype(BF16), g, i)

    def query_side(i):
        spread(groups + i - 2)
        rows = tile(i, PAIR * TOK)
        keys = gath[...].reshape(WIDTH, n_keys)
        low = dot_nn(keys, dst[:, rows]).astype(BF16)
        qlt[:, rows] = low
        weight_term(groups + i, low, qn, i)

    own_rows = TOK // n_head

    def key_side(k):
        cols = tile(k, TOK)
        value = dot_nn(pbt[cols, :], gl[...])
        key = dot_nn(dst[cols, :], qc[...])
        low = key[:, :D_LAT] + value
        gsend[:, k, :, :D_LAT] = low.reshape(n_head, own_rows, D_LAT).astype(BF16)
        gsend[:, k, :, D_LAT:] = key[:, D_LAT:].reshape(n_head, own_rows, D_ROPE).astype(BF16)

    each(0, groups, attend)
    each(0, groups, query_side)
    for i in range(2):
        each(i * n_ctx // 2, (i + 1) * n_ctx // 2, key_side)
        spread(pieces - 2 + i)
    h_keep = pltpu.make_async_copy(gsend.at[head], hrecv.at[n_head - 1], hown_s.at[0])
    h_keep.start()
    for k in range(1, n_head):
        h_copy(k).start()

    def nope(i):
        for sub in range(PAIR):
            rows = tile(i * PAIR + sub, 128)
            d_qn[0, :, rows] = dot_tn(qlt[:D_LAT, rows], wk[:, rows]).astype(BF16)

    def settle(p):
        z_keep(p).wait()
        total = zrecv[p, n_ctx - 1].astype(F32)
        for k in ctx_steps:
            z_copy(p, k).wait_recv()
            total = total + zrecv[p, k - 1].astype(F32)
        own[p] = total.astype(BF16)
        for k in ctx_steps:
            ag_copy(p, k).start()
        yag_copy(p, 0).start()
        own_keep(p).start()

    def hand_on(p):
        for k in ctx_steps:
            there = final.at[p, rep, ctx_at(-k)]
            copy(there, there, ag_s.at[p, k - 1], ag_r.at[p, k - 1],
                 (rep, ctx_at(k), head)).wait_recv()
            yag_copy(p, k).start()

    def latent_terms():
        h_keep.wait()
        for k in range(1, n_head):
            h_copy(k).wait_recv()
        for k in range(n_ctx):
            total = hrecv[n_head - 1, k].astype(F32)
            for i in range(n_head - 1):
                total = total + hrecv[i, k].astype(F32)
            if k == 0:
                d_lat[...] = total
            else:
                lsend[k - 1] = total.astype(BF16)
                l_copy(k).start()

    def settle_next(p):
        settle(p)
        hand_on(p - groups)

    each(0, groups, settle)
    each(0, groups, nope)
    for m in range(groups * PAIR):
        d_qr[0, :, m * D_ROPE:(m + 1) * D_ROPE] = qlt[D_LAT:, m * TOK:(m + 1) * TOK].T
    latent_terms()
    each(groups, pieces, settle_next)
    each(groups, pieces, hand_on)
    total = d_lat[...]
    for k in ctx_steps:
        l_copy(k).wait_recv()
        total = total + lrecv[k - 1].astype(F32)
    d_lat[...] = total

    for k in ctx_steps:
        lat_copy(k).wait_send()
        fwd_copy(k).wait_send()
        l_copy(k).wait_send()
    for k in range(1, n_head):
        h_copy(k).wait_send()

    def end(p):
        y_copy(p).wait_send()
        own_keep(p).wait()
        for k in ctx_steps:
            z_copy(p, k).wait_send()
            ag_copy(p, k).wait_send()
        for k in range(n_ctx):
            there = final.at[p, other, ctx_at(-k)]
            arrived = copy(there, there, yag_s.at[p, k], yag_r.at[p, k], (other, ctx, head))
            arrived.wait_recv()
            yag_copy(p, k).wait_send()

    each(0, pieces, end)


def finish(groups, lat, qn, qr, weights, d_lat, d_qn, d_qr, d_wk, d_wv):
    d_lat[0] = lat[...]
    d_qn[...] = qn[...]
    d_qr[...] = qr[...]
    for which, out in ((0, d_wv), (1, d_wk)):
        for i in range(groups):
            value = weights[which * groups + i].reshape(D_LAT, PAIR * 128)
            out[:, i * PAIR * 128:(i + 1) * PAIR * 128] = value.astype(F32)


def local(n_ctx, n_head, latent, q_nope, q_rope, grad_out, w_uk, w_uv, stretch_order):
    heads = w_uk.shape[1] // D_NOPE
    groups = heads // PAIR
    pieces = 2 * groups
    rows = heads * TOK
    n_keys = n_ctx * TOK
    own = TOK // n_head
    part = (D_LAT // (2 * n_ctx), PAIR * 128)
    vmem = pl.BlockSpec(memory_space=pltpu.VMEM)
    anywhere = pl.BlockSpec(memory_space=pl.ANY)
    dma = pltpu.SemaphoreType.DMA
    lat_out, qn_out, qr_out, weights = pl.pallas_call(
        functools.partial(body, n_ctx, n_head, groups),
        out_shape=(
            jax.ShapeDtypeStruct((own, WIDTH), F32),
            jax.ShapeDtypeStruct(q_nope.shape, BF16),
            jax.ShapeDtypeStruct(q_rope.shape, BF16),
            jax.ShapeDtypeStruct((pieces, 2, n_ctx) + part, BF16),
        ),
        in_specs=[anywhere] * 6 + [pl.BlockSpec(memory_space=pltpu.SMEM)],
        out_specs=(vmem,) * 4,
        scratch_shapes=[
            pltpu.VMEM(q_nope.shape, BF16),
            pltpu.VMEM(q_rope.shape, BF16),
            pltpu.VMEM(grad_out.shape, BF16),
            pltpu.VMEM(w_uk.shape, BF16),
            pltpu.VMEM(w_uv.shape, BF16),
            pltpu.VMEM((2, WIDTH // 2, n_keys), BF16),
            pltpu.VMEM((n_keys, WIDTH), BF16),
            pltpu.VMEM((rows, WIDTH), BF16),
            pltpu.VMEM((rows, D_LAT), BF16),
            pltpu.VMEM((WIDTH, rows), BF16),
            pltpu.VMEM((D_LAT, rows), BF16),
            pltpu.VMEM((WIDTH, rows), BF16),
            pltpu.VMEM((n_keys, PAIR * TOK), F32),
            pltpu.VMEM((n_keys, rows), BF16),
            pltpu.VMEM((n_keys, rows), BF16),
            pltpu.VMEM((pieces, 2, n_ctx) + part, BF16),
            pltpu.VMEM((pieces, n_ctx) + part, BF16),
            pltpu.VMEM((pieces, n_ctx) + part, BF16),
            pltpu.VMEM((pieces, n_ctx) + part, BF16),
            pltpu.VMEM((pieces, n_ctx) + part, BF16),
            pltpu.VMEM((pieces,) + part, BF16),
            pltpu.VMEM((n_head, n_ctx, own, WIDTH), BF16),
            pltpu.VMEM((n_head, n_ctx, own, WIDTH), BF16),
            pltpu.VMEM((n_ctx - 1, own, WIDTH), BF16),
            pltpu.VMEM((n_ctx - 1, own, WIDTH), BF16),
            dma((n_ctx - 1,)), dma((n_ctx - 1,)),
            dma((n_ctx - 1,)), dma((n_ctx - 1,)),
            dma((pieces,)), dma((pieces,)),
            dma((pieces, n_ctx - 1)), dma((pieces, n_ctx - 1)),
            dma((pieces, n_ctx - 1)), dma((pieces, n_ctx - 1)),
            dma((pieces, n_ctx)), dma((pieces, n_ctx)),
            dma((n_head - 1,)), dma((n_head - 1,)),
            dma((n_ctx - 1,)), dma((n_ctx - 1,)),
            dma((pieces,)), dma((pieces,)), dma((pieces,)), dma((1,)), dma((6,)),
        ],
        compiler_params=pltpu.CompilerParams(
            collective_id=0, has_side_effects=True, vmem_limit_bytes=56 << 20
        ),
    )(latent.transpose(0, 2, 1).reshape(2, WIDTH // 2, TOK), q_nope, q_rope, grad_out, w_uk, w_uv,
      stretch_order)
    return pl.pallas_call(
        functools.partial(finish, groups),
        out_shape=(
            jax.ShapeDtypeStruct((1, own, WIDTH), F32),
            jax.ShapeDtypeStruct(q_nope.shape, BF16),
            jax.ShapeDtypeStruct(q_rope.shape, BF16),
            jax.ShapeDtypeStruct(w_uk.shape, F32),
            jax.ShapeDtypeStruct(w_uv.shape, F32),
        ),
        in_specs=[vmem] * 4,
        out_specs=(vmem,) * 5,
        compiler_params=pltpu.CompilerParams(vmem_limit_bytes=60 << 20),
    )(lat_out, qn_out, qr_out, weights)


def solution(mesh):
    n_ctx, n_head = mesh.shape["ctx"], mesh.shape["head"]
    placed = (
        P("dp", "ctx", None),
        P("dp", "ctx", "head"),
        P("dp", "ctx", "head"),
        P("dp", "ctx", "head"),
        P(None, "head"),
        P(None, "head"),
        P(),
    )
    return jax.shard_map(
        functools.partial(local, n_ctx, n_head),
        mesh=mesh,
        in_specs=placed,
        out_specs=(
            P("dp", ("ctx", "head"), None),
            P("dp", "ctx", "head"),
            P("dp", "ctx", "head"),
            P(None, "head"),
            P(None, "head"),
        ),
        check_vma=False,
    )
```
